512 devices in a mesh: row: 16 (over y_hi, x), col: 32 (over y_lo, z, core).
Axes of the slice: x: 4, y: 8 (y_hi: 4, y_lo: 2; y = y_hi * 2 + y_lo), z: 8, core: 2. Of those that a mesh axis runs over, the one named last changes fastest.
Arguments:
- queries: bfloat16 [49152, 128], P(('row', 'col')), may hold values from -40 to 40
- keys: bfloat16 [49152, 128], P(('col', 'row')), may hold values from -4 to 4
- values: bfloat16 [49152, 128], P(('col', 'row')), may hold values from -6 to 6
- out_grad: bfloat16 [49152, 128], P(('row', 'col')), may hold values from -6 to 6
- unit_order: int32 [384], replicated, may hold values from 0 to 383, each once
Outputs:
- query_grad: bfloat16 [49152, 128], P(('row', 'col'))
- key_grad: bfloat16 [49152, 128], P(('col', 'row'))
- value_grad: bfloat16 [49152, 128], P(('col', 'row'))
The draws below stay inside these ranges and needn't reach their ends.
All inputs are finite; a program needn't handle non-finite values.
Results may differ from the reference program's by a relative error of at most 0.0051.
Values may be sent and summed in bfloat16 or wider, within the bound.
A program may use at most 128 MiB of HBM per device.

```python
import math
import jax
import jax.numpy as jnp
from jax import lax

HD = 128
UNIT = 128
TOKENS = 49152
UNITS = 384


def draw_keys(key, part):
    key = jax.random.fold_in(key, 2)
    result = jnp.clip(jax.random.normal(key, (TOKENS, HD), jnp.float32), -4.0, 4.0)
    return result.astype(jnp.bfloat16)


def draw_queries(key, part):
    key = jax.random.fold_in(key, 3)
    result = jnp.clip(jax.random.normal(key, (TOKENS, HD), jnp.float32), -6.0, 6.0)
    return result.astype(jnp.bfloat16)


def block_levels(own_key, dims, cuts, low, high):
    def one(dim, shards_of):
        heights = jax.random.uniform(jax.random.fold_in(jax.random.fold_in(own_key, 6), dim), (shards_of,), jnp.float32, low / len(cuts), high / len(cuts))
        return jnp.repeat(jnp.exp(heights), dims[dim] // shards_of).reshape((-1,) + (1,) * (len(dims) - dim - 1))

    gain = one(*cuts[0])
    for cut in cuts[1:]:
        gain = gain * one(*cut)
    return gain


def centred(own_key, extent, spread, reach, cuts=(), kind=jnp.bfloat16):
    array = spread * jax.random.normal(own_key, extent, jnp.float32)
    if cuts:
        array = array * block_levels(own_key, extent, cuts, -0.22, 0.18)
    return jnp.clip(array, -reach, reach).astype(kind)


def setup_inputs(seed: int = 0) -> dict:
    key_of = jax.random.split(jax.random.key(seed), 6)
    queries = draw_queries(jax.random.fold_in(key_of[5], 71), 0)
    keys = draw_keys(jax.random.fold_in(key_of[5], 71), 0)
    values = centred(key_of[2], (TOKENS, HD), 1.0, 6.0, ((0, 512),))
    out_grad = centred(key_of[3], (TOKENS, HD), 1.0, 6.0, ((0, 512),))
    unit_order = jax.random.permutation(key_of[4], UNITS).astype(jnp.int32)
    return dict(queries=queries, keys=keys, values=values, out_grad=out_grad, unit_order=unit_order)


masked_score = -1e+30

def token_positions(unit_order, count):
    index_rows = jnp.arange(count, dtype=jnp.int32)
    return (jnp.take(unit_order, index_rows // UNIT) * UNIT + index_rows % UNIT).astype(jnp.int32)

def reference(queries, keys, values, out_grad, unit_order):
    scale = 1.0 / math.sqrt(HD)
    positions = token_positions(unit_order, TOKENS)
    block_rows = math.gcd(TOKENS, 512)
    block_count = TOKENS // block_rows
    query_blocks = queries.reshape(block_count, block_rows, HD)
    grad_blocks = out_grad.reshape(block_count, block_rows, HD)
    position_blocks = positions.reshape(block_count, block_rows)
    contract_last = (((1,), (1,)), ((), ()))
    contract_first = (((0,), (0,)), ((), ()))

    def step(carry, item):
        key_acc, value_acc = carry
        query_rows, grad_rows, query_pos = item
        visible = positions[None, :] <= query_pos[:, None]
        scores = lax.dot_general(query_rows, keys, contract_last, preferred_element_type=jnp.float32) * scale
        scores = jnp.where(visible, scores, masked_score)
        peak_value = lax.optimization_barrier(jnp.max(scores, axis=1))
        total = lax.optimization_barrier(jnp.sum(jnp.where(visible, jnp.exp(scores - peak_value[:, None]), 0.0), axis=1))
        weights = jnp.where(visible, jnp.exp(scores - (peak_value + jnp.log(total))[:, None]), 0.0)
        grad_weights = lax.dot_general(grad_rows, values, contract_last, preferred_element_type=jnp.float32)
        row_dot = lax.optimization_barrier(jnp.sum(weights * grad_weights, axis=1))
        grad_scores = (weights * (grad_weights - row_dot[:, None]) * scale).astype(jnp.bfloat16)
        query_part = jnp.dot(grad_scores, keys, preferred_element_type=jnp.float32).astype(jnp.bfloat16)
        key_acc = key_acc + lax.dot_general(grad_scores, query_rows, contract_first, preferred_element_type=jnp.float32)
        value_acc = value_acc + lax.dot_general(weights.astype(jnp.bfloat16), grad_rows, contract_first, preferred_element_type=jnp.float32)
        return ((key_acc, value_acc), query_part)
    start = (jnp.zeros((TOKENS, HD), jnp.float32), jnp.zeros((TOKENS, HD), jnp.float32))
    (key_acc, value_acc), query_parts = lax.scan(step, start, (query_blocks, grad_blocks, position_blocks))
    query_grad = query_parts.reshape(TOKENS, HD)
    return (query_grad, key_acc.astype(jnp.bfloat16), value_acc.astype(jnp.bfloat16))
```

```python
import functools
import math

import jax
import jax.numpy as jnp
from jax import lax
from jax.experimental import pallas as pl
from jax.experimental.pallas import tpu as pltpu
from jax.sharding import PartitionSpec as P

UNIT = 128
HD = 128
SHARD = 96
YH, X, YL, Z, CORE = 4, 4, 2, 8, 2
ROWS, COLS = YH * X, YL * Z * CORE
QN, KN = COLS * SHARD, ROWS * SHARD
QUNITS, KUNITS = QN // UNIT, KN // UNIT
QT = 768
QTILES = QN // QT
CHUNK = 256
KT = 768
OWNERS = 8
PER_OWNER = QUNITS // OWNERS
SCALE = 1.0 / math.sqrt(HD)
LOG2_SCALE = math.log2(math.e) * SCALE
masked_score = -1e30
lowest_peak = -1e29
least_total = 1e-30

f32 = jnp.float32
bf16 = jnp.bfloat16
MESH = pl.DeviceIdType.MESH
contract_last = (((1,), (1,)), ((), ()))
contract_first = (((0,), (0,)), ((), ()))


def owner_col(o):
    return (o % 2) * (Z * CORE) + o * CORE + (o // 2) % 2


def kernel(
    q_ref, k_ref, v_ref, g_ref, units,
    dq_out, dk_out, dv_out,
    qd, kv, p_s, gw_s, peak_s, stat, inbox, result, done_stat,
    dq_acc, dkv_acc, sib_in, q_sum, zs, zr, ys, yr, xs0, xr0, xs1, xr1, kv_sum, hs, hr,
    y_ss, y_rs, z_ss, z_rs, c_ss, c_rs, h_ss, h_rs, x_ss, x_rs,
    a_ss, a_rs, b_ss, b_rs,
    rc_ss, rc_rs, rz_ss, rz_rs, ry_ss, ry_rs, rx_ss, rx_rs, rh_ss, rh_rs,
):
    r = lax.axis_index("row")
    c = lax.axis_index("col")
    yh, x = r // X, r % X
    yl, z, co = c // (Z * CORE), (c // CORE) % Z, c % CORE

    def col_of(a, b, d):
        return a * (Z * CORE) + b * CORE + d

    def row_of(a, b):
        return a * X + b

    def wrap(value, size):
        return lax.rem(value + size, size)

    sibling = (r, col_of(yl, z, 1 - co))
    y_peer = (r, col_of(1 - yl, z, co))
    z_next = [(r, col_of(yl, wrap(z + 1, Z), co)), (r, col_of(yl, wrap(z - 1, Z), co))]
    x_next = [(row_of(yh, wrap(x + 1, X)), c), (row_of(yh, wrap(x - 1, X)), c)]
    way = (1, -1)

    def send(src, dst, send_sem, recv_sem, device):
        copy = pltpu.make_async_remote_copy(
            src_ref=src, dst_ref=dst, send_sem=send_sem, recv_sem=recv_sem,
            device_id=device, device_id_type=MESH,
        )
        copy.start()
        return copy

    def arrive(dst, recv_sem):
        pltpu.make_async_remote_copy(
            src_ref=dst, dst_ref=dst, send_sem=recv_sem, recv_sem=recv_sem,
            device_id=sibling, device_id_type=MESH,
        ).wait_recv()

    barrier = pltpu.get_barrier_semaphore()

    def greet(other, _):
        @pl.when(other != c)
        def _():
            pl.semaphore_signal(barrier, inc=1, device_id=(r, other), device_id_type=MESH)
        return 0

    lax.fori_loop(0, COLS, greet, 0)
    for device in x_next:
        pl.semaphore_signal(barrier, inc=1, device_id=device, device_id_type=MESH)
    for j in range(1, YH):
        pl.semaphore_signal(
            barrier, inc=1, device_id=(row_of(wrap(yh + j, YH), x), c), device_id_type=MESH
        )

    def q_slot(col):
        return qd.at[:, pl.ds(pl.multiple_of(col * SHARD, SHARD), SHARD), :]

    def k_slot(row):
        return kv.at[:, pl.ds(pl.multiple_of(row * SHARD, SHARD), SHARD), :]

    own_q = pl.ds(pl.multiple_of(c * SHARD, SHARD), SHARD)
    own_k = pl.ds(pl.multiple_of(r * SHARD, SHARD), SHARD)
    qd[0, own_q, :] = q_ref[...]
    qd[1, own_q, :] = g_ref[...]
    kv[0, own_k, :] = k_ref[...]
    kv[1, own_k, :] = v_ref[...]
    pl.semaphore_wait(barrier, COLS - 1 + 2 + YH - 1)

    sent = []

    def ring_send(d, t, side, slot):
        sent.append(send(slot, slot, z_ss.at[d, t, side], z_rs.at[d, t, side], z_next[d]))

    def core_send(side, zz):
        slot = q_slot(col_of(side, zz, co))
        sent.append(send(slot, slot, c_ss.at[side, zz], c_rs.at[side, zz], sibling))

    def x_send(d, t, high, slot):
        sent.append(send(slot, slot, x_ss.at[d, t, high], x_rs.at[d, t, high], x_next[d]))

    mine = q_slot(c)
    mine_k = k_slot(r)
    sent.append(send(mine, mine, y_ss, y_rs, y_peer))
    for j in range(1, YH):
        sent.append(
            send(mine_k, mine_k, h_ss.at[j], h_rs.at[j], (row_of(wrap(yh + j, YH), x), c))
        )
    for d in range(2):
        ring_send(d, 0, yl, mine)
    for d in range(2):
        x_send(d, 0, yh, mine_k)
    core_send(yl, z)
    other = q_slot(col_of(1 - yl, z, co))
    arrive(other, y_rs)
    for d in range(2):
        ring_send(d, 0, 1 - yl, other)
    core_send(1 - yl, z)
    for j in range(1, YH):
        high = wrap(yh - j, YH)
        slot = k_slot(row_of(high, x))
        arrive(slot, h_rs.at[j])
        for d in range(2):
            x_send(d, 0, high, slot)

    def ring_arrive(t, side, d):
        zz = wrap(z - way[d] * (t + 1), Z)
        slot = q_slot(col_of(side, zz, co))
        arrive(slot, z_rs.at[d, t, side])
        if t < 2 or (t == 2 and side == d):
            ring_send(d, t + 1, side, slot)
        core_send(side, zz)

    def x_arrive(t, high, d):
        slot = k_slot(row_of(high, wrap(x - way[d] * (t + 1), X)))
        arrive(slot, x_rs.at[d, t, high])
        if t == 0 and high // 2 == d:
            x_send(d, 1, high, slot)

    for t in range(4):
        for side in range(2):
            for d in range(2):
                if t < 3 or side == d:
                    ring_arrive(t, side, d)
        if t < 2:
            for high in range(YH):
                for d in range(2):
                    if t == 0 or high // 2 == d:
                        x_arrive(t, high, d)
    for side in range(2):
        for zz in range(Z):
            arrive(q_slot(col_of(side, zz, 1 - co)), c_rs.at[side, zz])
    for copy in sent:
        copy.wait_send()

    def pass_1(qt):
        sub = lax.broadcasted_iota(jnp.int32, (UNIT, CHUNK), 0)
        lane = lax.broadcasted_iota(jnp.int32, (1, CHUNK), 1)

        def chunk(i, _):
            n = qt * (QT // CHUNK) + i
            at = pl.ds(pl.multiple_of(n * CHUNK, CHUNK), CHUNK)
            query, grad = qd[0, at, :], qd[1, at, :]
            first = r * QUNITS + n * 2
            query_pos = jnp.where(
                lane < UNIT, units[first] * UNIT + lane, units[first + 1] * UNIT + lane - UNIT
            )
            peaks, totals, dots = [], [], []
            for u in range(KUNITS):
                rows = slice(u * UNIT, (u + 1) * UNIT)
                scores = lax.dot_general(
                    kv[0, rows, :], query, contract_last, preferred_element_type=f32
                )
                grad_weights = lax.dot_general(
                    kv[1, rows, :], grad, contract_last, preferred_element_type=f32
                )
                visible = sub <= query_pos - units[c * KUNITS + u] * UNIT
                scores = jnp.where(visible, scores * LOG2_SCALE, masked_score)
                scores = scores.reshape(UNIT // 8, 8, CHUNK)
                peak = jnp.maximum(jnp.max(scores, axis=0), lowest_peak)
                expos = jnp.exp2(scores - peak[None])
                peaks.append(peak)
                totals.append(jnp.sum(expos, axis=0))
                dots.append(
                    jnp.sum(expos * grad_weights.reshape(UNIT // 8, 8, CHUNK), axis=0)
                )
                p_s[rows, at] = expos.reshape(UNIT, CHUNK)
                gw_s[rows, at] = grad_weights
                peak_s[u, :, at] = peak
            peak = jnp.max(functools.reduce(jnp.maximum, peaks), axis=0, keepdims=True)
            factors = [jnp.exp2(part - peak) for part in peaks]
            total = sum(a * b for a, b in zip(totals, factors))
            dot = sum(a * b for a, b in zip(dots, factors))
            total = jnp.maximum(jnp.sum(total, axis=0, keepdims=True), least_total)
            dot = jnp.sum(dot, axis=0, keepdims=True)
            lse = peak + jnp.log2(total)
            row_dot = dot / total
            for half in range(2):
                unit = n * 2 + half
                o, place = unit // PER_OWNER, unit % PER_OWNER
                lanes = slice(half * UNIT, (half + 1) * UNIT)
                stat[o, pl.ds(place, 1), :] = lse[:, lanes]
                stat[o, pl.ds(PER_OWNER + place, 1), :] = row_dot[:, lanes]
            return 0

        lax.fori_loop(0, QT // CHUNK, chunk, 0)

    tile_owners = OWNERS // QTILES

    def stat_send(qt):
        for o in range(tile_owners * qt, tile_owners * (qt + 1)):
            target = owner_col(o)

            @pl.when(target != c)
            def _():
                send(stat.at[o], inbox.at[c], a_ss.at[o], a_rs.at[c], (r, target))

            @pl.when(target == c)
            def _():
                inbox[c] = stat[o]

    def stat_combine(qt):
        for o in range(tile_owners * qt, tile_owners * (qt + 1)):
            target = owner_col(o)

            @pl.when(target != c)
            def _():
                pltpu.make_async_remote_copy(
                    src_ref=stat.at[o], dst_ref=inbox.at[c], send_sem=a_ss.at[o],
                    recv_sem=a_rs.at[c], device_id=(r, target), device_id_type=MESH,
                ).wait_send()

            @pl.when(target == c)
            def _():
                def take(other, _):
                    @pl.when(other != c)
                    def _():
                        arrive(inbox.at[other], a_rs.at[other])
                    return 0

                lax.fori_loop(0, COLS, take, 0)
                lse = inbox[:, 0:PER_OWNER, :]
                row_dot = inbox[:, PER_OWNER:2 * PER_OWNER, :]
                peak = jnp.max(lse, axis=0)
                part = jnp.exp2(lse - peak[None])
                total = jnp.sum(part, axis=0)
                result[0:PER_OWNER, :] = peak + jnp.log2(total)
                result[PER_OWNER:2 * PER_OWNER, :] = jnp.sum(part * row_dot, axis=0) / total
                done_stat[o] = result[...]

                def give(other, _):
                    @pl.when(other != c)
                    def _():
                        send(result, done_stat.at[o], b_ss.at[other], b_rs.at[o], (r, other))
                    return 0

                lax.fori_loop(0, COLS, give, 0)

                def given(other, _):
                    @pl.when(other != c)
                    def _():
                        pltpu.make_async_remote_copy(
                            src_ref=result, dst_ref=done_stat.at[o], send_sem=b_ss.at[other],
                            recv_sem=b_rs.at[o], device_id=(r, other), device_id_type=MESH,
                        ).wait_send()
                    return 0

                lax.fori_loop(0, COLS, given, 0)

    def stat_take(qt):
        for o in range(tile_owners * qt, tile_owners * (qt + 1)):
            @pl.when(owner_col(o) != c)
            def _():
                arrive(done_stat.at[o], b_rs.at[o])

    def pass_2(qt):
        at = slice(qt * QT, (qt + 1) * QT)
        lse, row_dot = [], []
        for o in range(tile_owners * qt, tile_owners * (qt + 1)):
            for i in range(PER_OWNER):
                lse.append(done_stat[o, i:i + 1, :])
                row_dot.append(done_stat[o, PER_OWNER + i:PER_OWNER + i + 1, :])
        lse, row_dot = jnp.concatenate(lse, axis=1), jnp.concatenate(row_dot, axis=1)

        def part(kt, _):
            weights, grad_scores = [], []
            for u in range(KT // UNIT):
                rows = pl.ds(pl.multiple_of(kt * KT + u * UNIT, UNIT), UNIT)
                factor = jnp.exp2(peak_s[kt * (KT // UNIT) + u, :, at] - lse)
                w = p_s[rows, at].reshape(UNIT // 8, 8, QT) * factor[None]
                g = w * (gw_s[rows, at].reshape(UNIT // 8, 8, QT) - row_dot[None])
                weights.append(w.reshape(UNIT, QT).astype(bf16))
                grad_scores.append(g.reshape(UNIT, QT).astype(bf16))
            weights = jnp.concatenate(weights, axis=0)
            grad_scores = jnp.concatenate(grad_scores, axis=0)
            highs = KT // (X * SHARD)
            shape = (highs, X, SHARD, HD)
            place = pl.ds(kt * highs, highs)
            value_part = jnp.dot(weights, qd[1, at, :], preferred_element_type=f32)
            key_part = jnp.dot(grad_scores, qd[0, at, :], preferred_element_type=f32)
            query_part = lax.dot_general(
                grad_scores, kv[0, pl.ds(pl.multiple_of(kt * KT, KT), KT), :], contract_first,
                preferred_element_type=f32,
            )
            dkv_acc[1, place] += value_part.reshape(shape)
            dkv_acc[0, place] += key_part.reshape(shape)
            pairs = QT // (CORE * SHARD)
            dq_acc[qt * pairs:(qt + 1) * pairs] += query_part.reshape(pairs, CORE, SHARD, HD)
            return 0

        lax.fori_loop(0, KN // KT, part, 0)

    dq_acc[...] = jnp.zeros_like(dq_acc)
    dkv_acc[...] = jnp.zeros_like(dkv_acc)
    result[...] = jnp.zeros_like(result)
    stat[...] = jnp.zeros_like(stat)
    for qt in range(QTILES):
        pass_1(qt)
        stat_send(qt)
        if qt > 0:
            stat_combine(qt - 1)
    for qt in range(QTILES):
        stat_take(qt)
        pass_2(qt)
        if qt == 0:
            stat_combine(QTILES - 1)

    sent = []

    def x_start(d):
        pair = slice(2 * d, 2 * d + 2)
        far = wrap(x + 2, X)
        for a in range(2):
            for i in range(2):
                xs0[d, a, i] = (dkv_acc[a, 2 * d + i, far] * (SCALE if a == 0 else 1.0)).astype(bf16)
        sent.append(send(xs0.at[d], xr0.at[d], rx_ss.at[d, 0], rx_rs.at[d, 0], x_next[d]))

    def x_middle(d):
        near = wrap(x + way[d], X)
        arrive(xr0.at[d], rx_rs.at[d, 0])
        for a in range(2):
            for high in range(YH):
                term = dkv_acc[a, high, near] * (SCALE if a == 0 else 1.0)
                if high // 2 == d:
                    term += xr0[d, a, high % 2].astype(f32)
                xs1[d, a, high] = term.astype(bf16)
        sent.append(send(xs1.at[d], xr1.at[d], rx_ss.at[d, 1], rx_rs.at[d, 1], x_next[d]))

    def x_end():
        for d in range(2):
            arrive(xr1.at[d], rx_rs.at[d, 1])
        for a in range(2):
            for high in range(YH):
                kv_sum[a, high] = (
                    dkv_acc[a, high, x] * (SCALE if a == 0 else 1.0)
                    + xr1[0, a, high].astype(f32) + xr1[1, a, high].astype(f32)
                )
        for j in range(1, YH):
            to = wrap(yh + j, YH)
            for a in range(2):
                hs[j, a] = kv_sum[a, to].astype(bf16)
            sent.append(send(hs.at[j], hr.at[j], rh_ss.at[j], rh_rs.at[j], (row_of(to, x), c)))

    def high_end():
        for j in range(1, YH):
            arrive(hr.at[j], rh_rs.at[j])
        for a, out in ((0, dk_out), (1, dv_out)):
            total = kv_sum[a, yh]
            for j in range(1, YH):
                total += hr[j, a].astype(f32)
            out[...] = total.astype(bf16)

    def core_start():
        sent.append(send(dq_acc.at[:, 1 - co], sib_in, rc_ss, rc_rs, sibling))

    def core_end():
        arrive(sib_in, rc_rs)
        for i in range(YL * Z):
            q_sum[i // Z, i % Z] = (dq_acc[i, co] + sib_in[i]) * SCALE

    def z_step(t):
        for d in range(2):
            for side in range(2):
                if t == 0 and side != d:
                    continue
                term = q_sum[side, wrap(z + way[d] * (4 - t), Z)]
                if t > 1 or (t == 1 and side == d):
                    arrive(zr.at[d, t - 1, side], rz_rs.at[d, t - 1, side])
                    term += zr[d, t - 1, side].astype(f32)
                zs[d, t, side] = term.astype(bf16)
                sent.append(
                    send(zs.at[d, t, side], zr.at[d, t, side], rz_ss.at[d, t, side],
                         rz_rs.at[d, t, side], z_next[d])
                )

    def z_end():
        for side in range(2):
            term = q_sum[side, z]
            for d in range(2):
                arrive(zr.at[d, 3, side], rz_rs.at[d, 3, side])
                term += zr[d, 3, side].astype(f32)
            q_sum[side, z] = term
        ys[...] = q_sum[1 - yl, z].astype(bf16)
        sent.append(send(ys, yr, ry_ss, ry_rs, y_peer))

    def y_end():
        arrive(yr, ry_rs)
        dq_out[...] = (q_sum[yl, z] + yr[...].astype(f32)).astype(bf16)

    core_start()
    x_start(0)
    x_start(1)
    core_end()
    z_step(0)
    z_step(1)
    x_middle(0)
    x_middle(1)
    z_step(2)
    z_step(3)
    x_end()
    z_end()
    y_end()
    high_end()
    for copy in sent:
        copy.wait_send()


def shards(queries, keys, values, out_grad, unit_order):
    vmem = pl.BlockSpec(memory_space=pltpu.VMEM)
    dma = pltpu.SemaphoreType.DMA
    shard = jax.ShapeDtypeStruct((SHARD, HD), bf16)
    tile = (SHARD, HD)
    return pl.pallas_call(
        kernel,
        out_shape=(shard, shard, shard),
        in_specs=[vmem] * 4 + [pl.BlockSpec(memory_space=pltpu.SMEM)],
        out_specs=(vmem, vmem, vmem),
        scratch_shapes=[
            pltpu.VMEM((2, QN, HD), bf16),
            pltpu.VMEM((2, KN, HD), bf16),
            pltpu.VMEM((KN, QN), f32),
            pltpu.VMEM((KN, QN), f32),
            pltpu.VMEM((KUNITS, 8, QN), f32),
            pltpu.VMEM((OWNERS, 8, UNIT), f32),
            pltpu.VMEM((COLS, 8, UNIT), f32),
            pltpu.VMEM((8, UNIT), f32),
            pltpu.VMEM((OWNERS, 8, UNIT), f32),
            pltpu.VMEM((YL * Z, CORE) + tile, f32),
            pltpu.VMEM((2, YH, X) + tile, f32),
            pltpu.VMEM((YL * Z,) + tile, f32),
            pltpu.VMEM((YL, Z) + tile, f32),
            pltpu.VMEM((2, 4, 2) + tile, bf16),
            pltpu.VMEM((2, 4, 2) + tile, bf16),
            pltpu.VMEM(tile, bf16),
            pltpu.VMEM(tile, bf16),
            pltpu.VMEM((2, 2, 2) + tile, bf16),
            pltpu.VMEM((2, 2, 2) + tile, bf16),
            pltpu.VMEM((2, 2, YH) + tile, bf16),
            pltpu.VMEM((2, 2, YH) + tile, bf16),
            pltpu.VMEM((2, YH) + tile, f32),
            pltpu.VMEM((YH, 2) + tile, bf16),
            pltpu.VMEM((YH, 2) + tile, bf16),
            dma, dma,
            dma((2, 4, 2)), dma((2, 4, 2)),
            dma((YL, Z)), dma((YL, Z)),
            dma((YH,)), dma((YH,)),
            dma((2, 2, YH)), dma((2, 2, YH)),
            dma((OWNERS,)), dma((COLS,)),
            dma((COLS,)), dma((OWNERS,)),
            dma, dma,
            dma((2, 4, 2)), dma((2, 4, 2)),
            dma, dma,
            dma((2, 2)), dma((2, 2)),
            dma((YH,)), dma((YH,)),
        ],
        compiler_params=pltpu.CompilerParams(
            collective_id=0, has_side_effects=True, vmem_limit_bytes=60 * 2**20
        ),
    )(queries, keys, values, out_grad, unit_order)


def solution(mesh):
    placed = (
        P(("row", "col"), None),
        P(("col", "row"), None),
        P(("col", "row"), None),
        P(("row", "col"), None),
        P(),
    )
    return jax.shard_map(
        shards,
        mesh=mesh,
        in_specs=placed,
        out_specs=(P(("row", "col"), None), P(("col", "row"), None), P(("col", "row"), None)),
        check_vma=False,
    )
```

```python
import functools
import math

import jax
import jax.numpy as jnp
from jax import lax
from jax.experimental import pallas as pl
from jax.experimental.pallas import tpu as pltpu
from jax.sharding import PartitionSpec as P

UNIT = 128
HD = 128
SHARD = 96
YH, X, YL, Z, CORE = 4, 4, 2, 8, 2
ROWS, COLS = YH * X, YL * Z * CORE
QN, KN = COLS * SHARD, ROWS * SHARD
QUNITS, KUNITS = QN // UNIT, KN // UNIT
QT = YL * CORE * SHARD
KT = X * SHARD
LANE_ROWS = QT // UNIT
MASK_ROWS = 32
SCALE = 1.0 / math.sqrt(HD)
LOG2_SCALE = math.log2(math.e) * SCALE
masked_score = -1e30
lowest_peak = -1e29
least_total = 1e-30

f32 = jnp.float32
bf16 = jnp.bfloat16
MESH = pl.DeviceIdType.MESH
contract_last = (((1,), (1,)), ((), ()))
contract_first = (((0,), (0,)), ((), ()))


def wrap(value, size):
    return lax.rem(value + size, size)


def owner_col(o):
    far = (o + Z // 2) % Z
    return (o % 2) * (Z * CORE) + far * CORE + (o // 2) % 2


def place_queries(units, r, pos_s):
    lane = lax.broadcasted_iota(jnp.int32, (8, QT), 1)
    half = CORE * SHARD
    side = lane // half
    for zz in range(Z):
        token = side * (Z * half) + zz * half + (lane - side * half)
        unit, inside = token // UNIT, token % UNIT
        base = jnp.zeros((8, QT), jnp.int32)
        for a in range(YL):
            first = (a * Z + zz) * half // UNIT
            for u in (first, first + 1):
                base = jnp.where(unit == u, units[r * QUNITS + u], base)
        pos_s[zz] = base * UNIT + inside


def pass_1_tile(units, c, zq, yk, qd, kv, pos_s, p_s, gw_s, peak_s, total_s, dot_s):
    query, grad = qd[0, zq].reshape(QT, HD), qd[1, zq].reshape(QT, HD)
    sub = lax.broadcasted_iota(jnp.int32, (MASK_ROWS // 8, 8, QT), 0) * 8 + lax.broadcasted_iota(
        jnp.int32, (MASK_ROWS // 8, 8, QT), 1
    )
    query_pos = pos_s[zq]
    keys, values = kv[0, yk].reshape(KT, HD), kv[1, yk].reshape(KT, HD)
    all_scores = lax.dot_general(keys, query, contract_last, preferred_element_type=f32)
    all_grads = lax.dot_general(values, grad, contract_last, preferred_element_type=f32)
    for place in range(X):
        rows = slice(place * SHARD, (place + 1) * SHARD)
        scores = all_scores[rows].reshape(SHARD // 8, 8, QT)
        grad_weights = all_grads[rows]
        parts = []
        for b in range(SHARD // MASK_ROWS):
            token = (yk * X + place) * SHARD + b * MASK_ROWS
            key_pos = units[c * KUNITS + token // UNIT] * UNIT + token % UNIT
            part = scores[b * MASK_ROWS // 8:(b + 1) * MASK_ROWS // 8]
            parts.append(
                jnp.where(sub <= (query_pos - key_pos)[None], part * LOG2_SCALE, masked_score)
            )
        scores = jnp.concatenate(parts, axis=0)
        peak = jnp.maximum(jnp.max(scores, axis=0), lowest_peak)
        expos = jnp.exp2(scores - peak[None])
        peak_s[zq, yk, place] = peak
        total_s[zq, yk, place] = jnp.sum(expos, axis=0)
        dot_s[zq, yk, place] = jnp.sum(expos * grad_weights.reshape(SHARD // 8, 8, QT), axis=0)
        p_s[zq, yk, rows, :] = expos.reshape(SHARD, QT)
        gw_s[zq, yk, rows, :] = grad_weights


def row_statistics(zq, peak_s, total_s, dot_s, stat):
    peaks = peak_s[zq].reshape(X * YH, 8, QT)
    peak = jnp.max(jnp.max(peaks, axis=0), axis=0, keepdims=True)
    factors = jnp.exp2(peaks - peak[None])
    total = jnp.sum(total_s[zq].reshape(X * YH, 8, QT) * factors, axis=0)
    dot = jnp.sum(dot_s[zq].reshape(X * YH, 8, QT) * factors, axis=0)
    total = jnp.maximum(jnp.sum(total, axis=0, keepdims=True), least_total)
    dot = jnp.sum(dot, axis=0, keepdims=True)
    lse = peak + jnp.log2(total)
    row_dot = dot / total
    for i in range(LANE_ROWS):
        lanes = slice(i * UNIT, (i + 1) * UNIT)
        stat[zq, i:i + 1, :] = lse[:, lanes]
        stat[zq, LANE_ROWS + i:LANE_ROWS + i + 1, :] = row_dot[:, lanes]


def pass_2_tile(zqs, yks, qd, kv, p_s, gw_s, peak_s, done_stat, dq_acc, dkv_acc, fresh=False):
    weights, grad_scores = [[] for _ in yks], [[] for _ in yks]
    for zq in zqs:
        lse = jnp.concatenate([done_stat[zq, i:i + 1, :] for i in range(LANE_ROWS)], axis=1)
        row_dot = jnp.concatenate(
            [done_stat[zq, LANE_ROWS + i:LANE_ROWS + i + 1, :] for i in range(LANE_ROWS)], axis=1
        )
        for j, yk in enumerate(yks):
            w_parts, g_parts = [], []
            for place in range(X):
                rows = slice(place * SHARD, (place + 1) * SHARD)
                factor = jnp.exp2(peak_s[zq, yk, place] - lse)
                w = p_s[zq, yk, rows, :].reshape(SHARD // 8, 8, QT) * factor[None]
                g = w * (gw_s[zq, yk, rows, :].reshape(SHARD // 8, 8, QT) - row_dot[None])
                w_parts.append(w.reshape(SHARD, QT).astype(bf16))
                g_parts.append(g.reshape(SHARD, QT).astype(bf16))
            weights[j].append(jnp.concatenate(w_parts, axis=0))
            grad_scores[j].append(jnp.concatenate(g_parts, axis=0))
    weights = [jnp.concatenate(row, axis=1) for row in weights]
    grad_scores = [jnp.concatenate(row, axis=1) for row in grad_scores]
    query = jnp.concatenate([qd[0, zq].reshape(QT, HD) for zq in zqs], axis=0)
    grad = jnp.concatenate([qd[1, zq].reshape(QT, HD) for zq in zqs], axis=0)
    for j, yk in enumerate(yks):
        value_part = jnp.dot(weights[j], grad, preferred_element_type=f32)
        key_part = jnp.dot(grad_scores[j], query, preferred_element_type=f32)
        dkv_acc[1, yk] += value_part.reshape(X, SHARD, HD)
        dkv_acc[0, yk] += key_part.reshape(X, SHARD, HD)
    query_part = lax.dot_general(
        jnp.concatenate(grad_scores, axis=0),
        jnp.concatenate([kv[0, yk].reshape(KT, HD) for yk in yks], axis=0),
        contract_first, preferred_element_type=f32,
    )
    for i, zq in enumerate(zqs):
        dq_acc[zq] += query_part[i * QT:(i + 1) * QT].reshape(YL, CORE, SHARD, HD)


def kernel(
    q_ref, k_ref, v_ref, g_ref, units,
    out,
    qd, kv, pos_s, p_s, gw_s, peak_s, total_s, dot_s, stat, inbox, result, done_stat,
    dq_acc, dkv_acc, sib_in, q_sum, zs, zr, ys, yr, xs, xr, kv_sum, hs, hr,
    y_ss, y_rs, z_ss, z_rs, n_ss, n_rs, c_ss, c_rs, h_ss, h_rs, x_ss, x_rs,
    a_ss, a_rs, b_ss, b_rs,
    own_s, rc_ss, rc_rs, rz_ss, rz_rs, ry_ss, ry_rs, rx_ss, rx_rs, rh_ss, rh_rs,
):
    r = lax.axis_index("row")
    c = lax.axis_index("col")
    yh, x = r // X, r % X
    yl, z, co = c // (Z * CORE), (c // CORE) % Z, c % CORE

    def col_of(a, b, d):
        return a * (Z * CORE) + b * CORE + d

    def row_of(a, b):
        return a * X + b

    def at_z(delta):
        return wrap(z + delta, Z)

    def at_x(delta):
        return wrap(x + delta, X)

    def at_y(delta):
        return wrap(yh + delta, YH)

    sibling = (r, col_of(yl, z, 1 - co))
    y_peer = (r, col_of(1 - yl, z, co))
    z_next = [(r, col_of(yl, at_z(1), co)), (r, col_of(yl, at_z(-1), co))]
    x_next = [(row_of(yh, at_x(1)), c), (row_of(yh, at_x(-1)), c), (row_of(yh, at_x(2)), c)]
    way = (1, -1)

    def send(src, dst, send_sem, recv_sem, device):
        copy = pltpu.make_async_remote_copy(
            src_ref=src, dst_ref=dst, send_sem=send_sem, recv_sem=recv_sem,
            device_id=device, device_id_type=MESH,
        )
        copy.start()
        return copy

    def arrive(dst, recv_sem):
        pltpu.make_async_remote_copy(
            src_ref=dst, dst_ref=dst, send_sem=recv_sem, recv_sem=recv_sem,
            device_id=sibling, device_id_type=MESH,
        ).wait_recv()

    barrier = pltpu.get_barrier_semaphore()

    def greet(other, _):
        @pl.when(other != c)
        def _():
            pl.semaphore_signal(barrier, inc=1, device_id=(r, other), device_id_type=MESH)
        return 0

    lax.fori_loop(0, COLS, greet, 0)
    for device in x_next:
        pl.semaphore_signal(barrier, inc=1, device_id=device, device_id_type=MESH)
    for j in range(1, YH):
        pl.semaphore_signal(
            barrier, inc=1, device_id=(row_of(at_y(j), x), c), device_id_type=MESH
        )

    own = [
        pltpu.make_async_copy(src, dst, own_s.at[i])
        for i, (src, dst) in enumerate((
            (q_ref, qd.at[0, z, yl, co]), (g_ref, qd.at[1, z, yl, co]),
            (k_ref, kv.at[0, yh, x]), (v_ref, kv.at[1, yh, x]),
        ))
    ]
    for copy in own:
        copy.start()

    def q_slot(a, b, d):
        return qd.at[:, b, a, d]

    def k_slot(high, xx):
        return kv.at[:, high, xx]

    for copy in own:
        copy.wait()
    pl.semaphore_wait(barrier, COLS - 1 + 3 + YH - 1)

    sent = []

    def core_send(side, zz):
        slot = q_slot(side, zz, co)
        sent.append(send(slot, slot, c_ss.at[side, zz], c_rs.at[side, zz], sibling))

    def x_sends(high, slot):
        for d in range(3):
            sent.append(send(slot, slot, x_ss.at[d, high], x_rs.at[d, high], x_next[d]))

    def z_arrive(*deltas):
        for delta in deltas:
            zz = at_z(delta)
            slot = q_slot(yl, zz, co)
            arrive(slot, z_rs.at[zz])
            if abs(delta) > 1:
                sent.append(send(slot, slot, y_ss.at[zz], y_rs.at[zz], y_peer))
            core_send(yl, zz)

    def y_arrive(*deltas):
        for delta in deltas:
            zz = at_z(delta)
            slot = q_slot(1 - yl, zz, co)
            arrive(slot, y_rs.at[zz])
            if delta == 0:
                for d in range(2):
                    sent.append(send(slot, slot, n_ss.at[d], n_rs.at[d], z_next[d]))
            core_send(1 - yl, zz)

    def near_arrive():
        for d in range(2):
            zz = at_z(-way[d])
            arrive(q_slot(1 - yl, zz, co), n_rs.at[d])
            core_send(1 - yl, zz)

    def h_arrive(j):
        high = at_y(-j)
        slot = k_slot(high, x)
        arrive(slot, h_rs.at[j])
        x_sends(high, slot)

    def x_arrive(delta):
        high = at_y(delta)
        for d in range(3):
            arrive(k_slot(high, at_x((-1, 1, 2)[d])), x_rs.at[d, high])

    def query_ready(zz):
        for side in range(2):
            arrive(q_slot(side, zz, 1 - co), c_rs.at[side, zz])

    def scores_of(count, where):
        def one(i, _):
            dz, dy = where(i)
            pass_1_tile(
                units, c, at_z(dz), at_y(dy), qd, kv, pos_s, p_s, gw_s, peak_s, total_s, dot_s
            )
            return 0

        lax.fori_loop(0, count, one, 0)

    def stat_send(*deltas):
        for delta in deltas:
            row_statistics(at_z(delta), peak_s, total_s, dot_s, stat)
        for delta in deltas:
            zq = at_z(delta)
            target = owner_col(zq)

            @pl.when(target != c)
            def _():
                send(stat.at[zq], inbox.at[c], a_ss.at[zq], a_rs.at[c], (r, target))

            @pl.when(target == c)
            def _():
                inbox[c] = stat[zq]

    mine = q_slot(yl, z, co)
    mine_k = k_slot(yh, x)
    sent.append(send(mine, mine, y_ss.at[z], y_rs.at[z], y_peer))
    for j in (1, 3, 2):
        sent.append(
            send(mine_k, mine_k, h_ss.at[j], h_rs.at[j], (row_of(at_y(j), x), c))
        )
    x_sends(yh, mine_k)
    for delta in (1, -1, 2, -2, 3, -3, 4):
        zz = at_z(delta)
        sent.append(
            send(mine, mine, z_ss.at[zz], z_rs.at[z], (r, col_of(yl, zz, co)))
        )
    core_send(yl, z)
    place_queries(units, r, pos_s)
    result[...] = jnp.zeros_like(result)
    stat[...] = jnp.zeros_like(stat)
    dq_acc[...] = jnp.zeros_like(dq_acc)
    dkv_acc[...] = jnp.zeros_like(dkv_acc)
    y_arrive(0)
    z_arrive(1, -1)
    x_arrive(0)
    query_ready(z)
    scores_of(1, lambda i: (i, 0))
    z_arrive(2, -2)
    h_arrive(1)
    h_arrive(3)
    near_arrive()
    query_ready(at_z(1))
    query_ready(at_z(-1))
    scores_of(2, lambda i: (2 * i - 1, 0))
    h_arrive(2)
    z_arrive(3, -3)
    y_arrive(2, -2)
    query_ready(at_z(2))
    query_ready(at_z(-2))
    scores_of(2, lambda i: (4 * i - 2, 0))
    z_arrive(4)
    x_arrive(-1)
    scores_of(5, lambda i: (i - 2, -1))
    y_arrive(3, -3)
    x_arrive(1)
    scores_of(5, lambda i: (i - 2, 1))
    query_ready(at_z(3))
    query_ready(at_z(-3))
    scores_of(6, lambda i: (6 * (i // 3) - 3, i % 3 - 1))
    y_arrive(4)
    query_ready(at_z(4))
    scores_of(3, lambda i: (4, i - 1))
    x_arrive(2)
    scores_of(4, lambda i: ((2 * (i % 2) - 1) * ((i + 1) // 2), 2))
    stat_send(0, 1, -1, 2)
    scores_of(4, lambda i: ((2 * (i % 2) - 1) * ((i + 5) // 2), 2))
    stat_send(-2, 3, -3, 4)

    def stat_sent(o, _):
        @pl.when(owner_col(o) != c)
        def _():
            pltpu.make_async_remote_copy(
                src_ref=stat.at[o], dst_ref=inbox.at[c], send_sem=a_ss.at[o],
                recv_sem=a_rs.at[c], device_id=(r, owner_col(o)), device_id_type=MESH,
            ).wait_send()
        return 0

    owned = at_z(4)
    partners = [
        (r, col_of(wrap(yl + a, YL), at_z(delta), wrap(co + b, CORE)))
        for delta in (4, 3, -3, 2, -2, 1, -1, 0) for a in (1, 0) for b in (1, 0)
        if (delta, a, b) != (0, 0, 0)
    ]

    def give(partner):
        return pltpu.make_async_remote_copy(
            src_ref=result, dst_ref=done_stat.at[owned], send_sem=b_ss.at[partner[1]],
            recv_sem=b_rs.at[owned], device_id=partner, device_id_type=MESH,
        )

    @pl.when(owner_col(owned) == c)
    def _():
        for partner in reversed(partners):
            arrive(inbox.at[partner[1]], a_rs.at[partner[1]])
        lse = inbox[:, 0:LANE_ROWS, :]
        row_dot = inbox[:, LANE_ROWS:2 * LANE_ROWS, :]
        peak = jnp.max(lse, axis=0)
        part = jnp.exp2(lse - peak[None])
        total = jnp.sum(part, axis=0)
        result[0:LANE_ROWS, :] = peak + jnp.log2(total)
        result[LANE_ROWS:2 * LANE_ROWS, :] = jnp.sum(part * row_dot, axis=0) / total
        for partner in partners:
            give(partner).start()
        done_stat[owned] = result[...]

    def stat_take(zq):
        @pl.when(owner_col(zq) != c)
        def _():
            arrive(done_stat.at[zq], b_rs.at[zq])

    gather_sent = sent
    sent = []

    def grads_of(zqs, yks):
        pass_2_tile(
            [at_z(d) for d in zqs], [at_y(d) for d in yks],
            qd, kv, p_s, gw_s, peak_s, done_stat, dq_acc, dkv_acc,
        )

    def core_start(zz):
        sent.append(
            send(dq_acc.at[zz, :, 1 - co], sib_in.at[zz], rc_ss.at[zz], rc_rs.at[zz], sibling)
        )

    def core_end(zz):
        arrive(sib_in.at[zz], rc_rs.at[zz])
        return (dq_acc[zz, :, co] + sib_in[zz]) * SCALE

    def z_send(zz):
        zs[zz] = core_end(zz).astype(bf16)
        sent.append(
            send(zs.at[zz], zr.at[z], rz_ss.at[zz], rz_rs.at[z], (r, col_of(yl, zz, co)))
        )

    def z_end():
        total = core_end(z)
        for delta in (4, 3, -3, 2, -2, 1, -1):
            zz = at_z(delta)
            arrive(zr.at[zz], rz_rs.at[zz])
            total += zr[zz].astype(f32)
        q_sum[...] = total
        ys[...] = q_sum[1 - yl].astype(bf16)
        sent.append(send(ys, yr, ry_ss, ry_rs, y_peer))

    def y_end():
        arrive(yr, ry_rs)
        out[0] = (q_sum[yl] + yr[...].astype(f32)).astype(bf16)

    def scaled(a):
        return SCALE if a == 0 else 1.0

    def column_send(dy):
        for d in range(3):
            for a in range(2):
                term = dkv_acc[a, at_y(dy), at_x((1, -1, 2)[d])] * scaled(a)
                xs[dy % YH, d, a] = term.astype(bf16)
            sent.append(
                send(xs.at[dy % YH, d], xr.at[dy % YH, d], rx_ss.at[dy % YH, d],
                     rx_rs.at[dy % YH, d], x_next[d])
            )

    def column_end(dy):
        for d in range(3):
            arrive(xr.at[dy % YH, d], rx_rs.at[dy % YH, d])
        for a in range(2):
            total = dkv_acc[a, at_y(dy), x] * scaled(a)
            for d in range(3):
                total += xr[dy % YH, d, a].astype(f32)
            if dy == 0:
                kv_sum[a] = total
            else:
                hs[dy % YH, a] = total.astype(bf16)
        if dy != 0:
            j = dy % YH
            sent.append(
                send(hs.at[j], hr.at[j], rh_ss.at[j], rh_rs.at[j], (row_of(at_y(dy), x), c))
            )

    def high_end():
        for j in range(1, YH):
            arrive(hr.at[j], rh_rs.at[j])
        for a in range(2):
            total = kv_sum[a]
            for j in range(1, YH):
                total += hr[j, a].astype(f32)
            out[1 + a] = total.astype(bf16)

    for pair in ((4, 3), (-3, 2), (-2, 1), (-1, 0)):
        for delta in pair:
            stat_take(at_z(delta))
        grads_of(pair, [2])
    column_send(2)
    grads_of([4], [1, -1])
    grads_of([4], [0])
    core_start(at_z(4))
    grads_of([3, -3], [1, -1])
    z_send(at_z(4))
    grads_of([3, -3], [0])
    core_start(at_z(3))
    core_start(at_z(-3))

    for dy in (1, -1):
        grads_of([2, -2], [dy])
        if dy == 1:
            z_send(at_z(3))
            z_send(at_z(-3))
        grads_of([1, -1], [dy])
        grads_of([0], [dy])
        column_send(dy)
    column_end(2)
    grads_of([2, -2], [0])
    core_start(at_z(2))
    core_start(at_z(-2))
    grads_of([1, -1], [0])
    core_start(at_z(1))
    core_start(at_z(-1))
    z_send(at_z(2))
    z_send(at_z(-2))
    grads_of([0], [0])
    core_start(z)
    column_send(0)
    z_send(at_z(1))
    z_send(at_z(-1))
    column_end(1)
    column_end(-1)
    z_end()
    column_end(0)
    y_end()
    high_end()
    for copy in gather_sent + sent:
        copy.wait_send()
    lax.fori_loop(0, Z, stat_sent, 0)

    @pl.when(owner_col(owned) == c)
    def _():
        for partner in partners:
            give(partner).wait_send()


def parted(whole, *parts):
    for i, part in enumerate(parts):
        part[...] = whole[i]


def shards(queries, keys, values, out_grad, unit_order):
    vmem = pl.BlockSpec(memory_space=pltpu.VMEM)
    dma = pltpu.SemaphoreType.DMA
    shard = jax.ShapeDtypeStruct((SHARD, HD), bf16)
    tile = (SHARD, HD)
    groups = (Z, YH, X, 8, QT)
    whole = pl.pallas_call(
        kernel,
        out_shape=jax.ShapeDtypeStruct((3, SHARD, HD), bf16),
        in_specs=[pl.BlockSpec(memory_space=pl.ANY)] * 4 + [pl.BlockSpec(memory_space=pltpu.SMEM)],
        out_specs=vmem,
        scratch_shapes=[
            pltpu.VMEM((2, Z, YL, CORE) + tile, bf16),
            pltpu.VMEM((2, YH, X) + tile, bf16),
            pltpu.VMEM((Z, 8, QT), jnp.int32),
            pltpu.VMEM((Z, YH, KT, QT), f32),
            pltpu.VMEM((Z, YH, KT, QT), f32),
            pltpu.VMEM(groups, f32),
            pltpu.VMEM(groups, f32),
            pltpu.VMEM(groups, f32),
            pltpu.VMEM((Z, 8, UNIT), f32),
            pltpu.VMEM((COLS, 8, UNIT), f32),
            pltpu.VMEM((8, UNIT), f32),
            pltpu.VMEM((Z, 8, UNIT), f32),
            pltpu.VMEM((Z, YL, CORE) + tile, f32),
            pltpu.VMEM((2, YH, X) + tile, f32),
            pltpu.VMEM((Z, YL) + tile, f32),
            pltpu.VMEM((YL,) + tile, f32),
            pltpu.VMEM((Z, YL) + tile, bf16),
            pltpu.VMEM((Z, YL) + tile, bf16),
            pltpu.VMEM(tile, bf16),
            pltpu.VMEM(tile, bf16),
            pltpu.VMEM((YH, 3, 2) + tile, bf16),
            pltpu.VMEM((YH, 3, 2) + tile, bf16),
            pltpu.VMEM((2,) + tile, f32),
            pltpu.VMEM((YH, 2) + tile, bf16),
            pltpu.VMEM((YH, 2) + tile, bf16),
            dma((Z,)), dma((Z,)),
            dma((Z,)), dma((Z,)),
            dma((2,)), dma((2,)),
            dma((YL, Z)), dma((YL, Z)),
            dma((YH,)), dma((YH,)),
            dma((3, YH)), dma((3, YH)),
            dma((Z,)), dma((COLS,)),
            dma((COLS,)), dma((Z,)),
            dma((4,)),
            dma((Z,)), dma((Z,)),
            dma((Z,)), dma((Z,)),
            dma, dma,
            dma((YH, 3)), dma((YH, 3)),
            dma((YH,)), dma((YH,)),
        ],
        compiler_params=pltpu.CompilerParams(
            collective_id=0, has_side_effects=True, vmem_limit_bytes=60 * 2**20
        ),
    )(queries, keys, values, out_grad, unit_order)
    return pl.pallas_call(
        parted,
        out_shape=(shard, shard, shard),
        in_specs=[vmem],
        out_specs=(vmem, vmem, vmem),
    )(whole)


def solution(mesh):
    placed = (
        P(("row", "col"), None),
        P(("col", "row"), None),
        P(("col", "row"), None),
        P(("row", "col"), None),
        P(),
    )
    return jax.shard_map(
        shards,
        mesh=mesh,
        in_specs=placed,
        out_specs=(P(("row", "col"), None), P(("col", "row"), None), P(("col", "row"), None)),
        check_vma=False,
    )
```

```python
import functools
import math

import jax
import jax.numpy as jnp
from jax import lax
from jax.experimental import pallas as pl
from jax.experimental.pallas import tpu as pltpu
from jax.sharding import PartitionSpec as P

UNIT = 128
HD = 128
SHARD = 96
YH, X, YL, Z, CORE = 4, 4, 2, 8, 2
ROWS, COLS = YH * X, YL * Z * CORE
QN, KN = COLS * SHARD, ROWS * SHARD
QUNITS, KUNITS = QN // UNIT, KN // UNIT
QT = YL * CORE * SHARD
KT = X * SHARD
LANE_ROWS = QT // UNIT
MASK_ROWS = 32
SCALE = 1.0 / math.sqrt(HD)
LOG2_SCALE = math.log2(math.e) * SCALE
masked_score = -1e30
lowest_peak = -1e29
least_total = 1e-30

f32 = jnp.float32
bf16 = jnp.bfloat16
MESH = pl.DeviceIdType.MESH
contract_last = (((1,), (1,)), ((), ()))
contract_first = (((0,), (0,)), ((), ()))


def wrap(value, size):
    return lax.rem(value + size, size)


def owner_col(o):
    far = (o + Z // 2) % Z
    return (o % 2) * (Z * CORE) + far * CORE + (o // 2) % 2


def place_queries(units, r, pos_s):
    lane = lax.broadcasted_iota(jnp.int32, (8, QT), 1)
    half = CORE * SHARD
    side = lane // half
    for zz in range(Z):
        token = side * (Z * half) + zz * half + (lane - side * half)
        unit, inside = token // UNIT, token % UNIT
        base = jnp.zeros((8, QT), jnp.int32)
        for a in range(YL):
            first = (a * Z + zz) * half // UNIT
            for u in (first, first + 1):
                base = jnp.where(unit == u, units[r * QUNITS + u], base)
        pos_s[zz] = base * UNIT + inside


def pass_1_tile(units, c, zq, yk, qd, kv, pos_s, p_s, gw_s, peak_s, total_s, dot_s):
    query, grad = qd[0, zq].reshape(QT, HD), qd[1, zq].reshape(QT, HD)
    sub = lax.broadcasted_iota(jnp.int32, (MASK_ROWS // 8, 8, QT), 0) * 8 + lax.broadcasted_iota(
        jnp.int32, (MASK_ROWS // 8, 8, QT), 1
    )
    query_pos = pos_s[zq]
    keys, values = kv[0, yk].reshape(KT, HD), kv[1, yk].reshape(KT, HD)
    all_scores = lax.dot_general(keys, query, contract_last, preferred_element_type=f32)
    all_grads = lax.dot_general(values, grad, contract_last, preferred_element_type=f32)
    for place in range(X):
        rows = slice(place * SHARD, (place + 1) * SHARD)
        scores = all_scores[rows].reshape(SHARD // 8, 8, QT)
        grad_weights = all_grads[rows]
        parts = []
        for b in range(SHARD // MASK_ROWS):
            token = (yk * X + place) * SHARD + b * MASK_ROWS
            key_pos = units[c * KUNITS + token // UNIT] * UNIT + token % UNIT
            part = scores[b * MASK_ROWS // 8:(b + 1) * MASK_ROWS // 8]
            parts.append(
                jnp.where(sub <= (query_pos - key_pos)[None], part * LOG2_SCALE, masked_score)
            )
        scores = jnp.concatenate(parts, axis=0)
        peak = jnp.maximum(jnp.max(scores, axis=0), lowest_peak)
        expos = jnp.exp2(scores - peak[None])
        peak_s[zq, yk, place] = peak
        total_s[zq, yk, place] = jnp.sum(expos, axis=0)
        dot_s[zq, yk, place] = jnp.sum(expos * grad_weights.reshape(SHARD // 8, 8, QT), axis=0)
        p_s[zq, yk, rows, :] = expos.reshape(SHARD, QT)
        gw_s[zq, yk, rows, :] = grad_weights


def row_statistics(zq, peak_s, total_s, dot_s, stat):
    peaks = peak_s[zq].reshape(X * YH, 8, QT)
    peak = jnp.max(jnp.max(peaks, axis=0), axis=0, keepdims=True)
    factors = jnp.exp2(peaks - peak[None])
    total = jnp.sum(total_s[zq].reshape(X * YH, 8, QT) * factors, axis=0)
    dot = jnp.sum(dot_s[zq].reshape(X * YH, 8, QT) * factors, axis=0)
    total = jnp.maximum(jnp.sum(total, axis=0, keepdims=True), least_total)
    dot = jnp.sum(dot, axis=0, keepdims=True)
    lse = peak + jnp.log2(total)
    row_dot = dot / total
    for i in range(LANE_ROWS):
        lanes = slice(i * UNIT, (i + 1) * UNIT)
        stat[zq, i:i + 1, :] = lse[:, lanes]
        stat[zq, LANE_ROWS + i:LANE_ROWS + i + 1, :] = row_dot[:, lanes]


def pass_2_tile(zqs, yks, qd, kv, p_s, gw_s, peak_s, done_stat, dq_acc, dkv_acc, fresh=False):
    weights, grad_scores = [[] for _ in yks], [[] for _ in yks]
    for zq in zqs:
        lse = jnp.concatenate([done_stat[zq, i:i + 1, :] for i in range(LANE_ROWS)], axis=1)
        row_dot = jnp.concatenate(
            [done_stat[zq, LANE_ROWS + i:LANE_ROWS + i + 1, :] for i in range(LANE_ROWS)], axis=1
        )
        for j, yk in enumerate(yks):
            w_parts, g_parts = [], []
            for place in range(X):
                rows = slice(place * SHARD, (place + 1) * SHARD)
                factor = jnp.exp2(peak_s[zq, yk, place] - lse)
                w = p_s[zq, yk, rows, :].reshape(SHARD // 8, 8, QT) * factor[None]
                g = w * (gw_s[zq, yk, rows, :].reshape(SHARD // 8, 8, QT) - row_dot[None])
                w_parts.append(w.reshape(SHARD, QT).astype(bf16))
                g_parts.append(g.reshape(SHARD, QT).astype(bf16))
            weights[j].append(jnp.concatenate(w_parts, axis=0))
            grad_scores[j].append(jnp.concatenate(g_parts, axis=0))
    weights = [jnp.concatenate(row, axis=1) for row in weights]
    grad_scores = [jnp.concatenate(row, axis=1) for row in grad_scores]
    query = jnp.concatenate([qd[0, zq].reshape(QT, HD) for zq in zqs], axis=0)
    grad = jnp.concatenate([qd[1, zq].reshape(QT, HD) for zq in zqs], axis=0)
    for j, yk in enumerate(yks):
        value_part = jnp.dot(weights[j], grad, preferred_element_type=f32)
        key_part = jnp.dot(grad_scores[j], query, preferred_element_type=f32)
        dkv_acc[1, yk] += value_part.reshape(X, SHARD, HD)
        dkv_acc[0, yk] += key_part.reshape(X, SHARD, HD)
    query_part = lax.dot_general(
        jnp.concatenate(grad_scores, axis=0),
        jnp.concatenate([kv[0, yk].reshape(KT, HD) for yk in yks], axis=0),
        contract_first, preferred_element_type=f32,
    )
    for i, zq in enumerate(zqs):
        dq_acc[zq] += query_part[i * QT:(i + 1) * QT].reshape(YL, CORE, SHARD, HD)


def kernel(
    q_ref, k_ref, v_ref, g_ref, units,
    out,
    qd, kv, pos_s, p_s, gw_s, peak_s, total_s, dot_s, stat, inbox, result, done_stat,
    dq_acc, dkv_acc, sib_in, q_sum, zs, zr, ys, yr, xs, xr, kv_sum, hs, hr,
    y_ss, y_rs, z_ss, z_rs, n_ss, n_rs, c_ss, c_rs, h_ss, h_rs, x_ss, x_rs,
    a_ss, a_rs, b_ss, b_rs,
    own_s, rc_ss, rc_rs, rz_ss, rz_rs, ry_ss, ry_rs, rx_ss, rx_rs, rh_ss, rh_rs,
):
    r = lax.axis_index("row")
    c = lax.axis_index("col")
    yh, x = r // X, r % X
    yl, z, co = c // (Z * CORE), (c // CORE) % Z, c % CORE

    def col_of(a, b, d):
        return a * (Z * CORE) + b * CORE + d

    def row_of(a, b):
        return a * X + b

    def at_z(delta):
        return wrap(z + delta, Z)

    def at_x(delta):
        return wrap(x + delta, X)

    def at_y(delta):
        return wrap(yh + delta, YH)

    sibling = (r, col_of(yl, z, 1 - co))
    y_peer = (r, col_of(1 - yl, z, co))
    z_next = [(r, col_of(yl, at_z(1), co)), (r, col_of(yl, at_z(-1), co))]
    x_next = [(row_of(yh, at_x(1)), c), (row_of(yh, at_x(-1)), c), (row_of(yh, at_x(2)), c)]
    way = (1, -1)

    def send(src, dst, send_sem, recv_sem, device):
        copy = pltpu.make_async_remote_copy(
            src_ref=src, dst_ref=dst, send_sem=send_sem, recv_sem=recv_sem,
            device_id=device, device_id_type=MESH,
        )
        copy.start()
        return copy

    def arrive(dst, recv_sem):
        pltpu.make_async_remote_copy(
            src_ref=dst, dst_ref=dst, send_sem=recv_sem, recv_sem=recv_sem,
            device_id=sibling, device_id_type=MESH,
        ).wait_recv()

    barrier = pltpu.get_barrier_semaphore()

    partners = [
        (r, col_of(wrap(yl + a, YL), at_z(delta), wrap(co + b, CORE)))
        for delta in (4, 3, -3, 2, -2, 1, -1, 0) for a in (1, 0) for b in (1, 0)
        if (delta, a, b) != (0, 0, 0)
    ]
    for device in partners:
        pl.semaphore_signal(barrier, inc=1, device_id=device, device_id_type=MESH)
    for device in x_next:
        pl.semaphore_signal(barrier, inc=1, device_id=device, device_id_type=MESH)
    for j in range(1, YH):
        pl.semaphore_signal(
            barrier, inc=1, device_id=(row_of(at_y(j), x), c), device_id_type=MESH
        )

    own = [
        pltpu.make_async_copy(src, dst, own_s.at[i])
        for i, (src, dst) in enumerate((
            (q_ref, qd.at[0, z, yl, co]), (g_ref, qd.at[1, z, yl, co]),
            (k_ref, kv.at[0, yh, x]), (v_ref, kv.at[1, yh, x]),
        ))
    ]
    for copy in own:
        copy.start()

    def q_slot(a, b, d):
        return qd.at[:, b, a, d]

    def k_slot(high, xx):
        return kv.at[:, high, xx]

    for copy in own:
        copy.wait()
    pl.semaphore_wait(barrier, COLS - 1 + 3 + YH - 1)

    sent = []

    def core_send(side, zz):
        slot = q_slot(side, zz, co)
        sent.append(send(slot, slot, c_ss.at[side, zz], c_rs.at[side, zz], sibling))

    def x_sends(high, slot):
        for d in range(3):
            sent.append(send(slot, slot, x_ss.at[d, high], x_rs.at[d, high], x_next[d]))

    def z_arrive(*deltas):
        for delta in deltas:
            zz = at_z(delta)
            slot = q_slot(yl, zz, co)
            arrive(slot, z_rs.at[zz])
            if abs(delta) > 1:
                sent.append(send(slot, slot, y_ss.at[zz], y_rs.at[zz], y_peer))
            core_send(yl, zz)

    def y_arrive(*deltas):
        for delta in deltas:
            zz = at_z(delta)
            slot = q_slot(1 - yl, zz, co)
            arrive(slot, y_rs.at[zz])
            if delta == 0:
                for d in range(2):
                    sent.append(send(slot, slot, n_ss.at[d], n_rs.at[d], z_next[d]))
            core_send(1 - yl, zz)

    def near_arrive():
        for d in range(2):
            zz = at_z(-way[d])
            arrive(q_slot(1 - yl, zz, co), n_rs.at[d])
            core_send(1 - yl, zz)

    def h_arrive(j):
        high = at_y(-j)
        slot = k_slot(high, x)
        arrive(slot, h_rs.at[j])
        x_sends(high, slot)

    def x_arrive(delta):
        high = at_y(delta)
        for d in range(3):
            arrive(k_slot(high, at_x((-1, 1, 2)[d])), x_rs.at[d, high])

    def query_ready(zz):
        for side in range(2):
            arrive(q_slot(side, zz, 1 - co), c_rs.at[side, zz])

    def scores_of(count, where):
        def one(i, _):
            dz, dy = where(i)
            pass_1_tile(
                units, c, at_z(dz), at_y(dy), qd, kv, pos_s, p_s, gw_s, peak_s, total_s, dot_s
            )
            return 0

        lax.fori_loop(0, count, one, 0, unroll=count)

    def stat_send(*deltas):
        for delta in deltas:
            row_statistics(at_z(delta), peak_s, total_s, dot_s, stat)
        for delta in deltas:
            zq = at_z(delta)
            target = owner_col(zq)

            @pl.when(target != c)
            def _():
                send(stat.at[zq], inbox.at[c], a_ss.at[zq], a_rs.at[c], (r, target))

            @pl.when(target == c)
            def _():
                inbox[c] = stat[zq]

    mine = q_slot(yl, z, co)
    mine_k = k_slot(yh, x)
    sent.append(send(mine, mine, y_ss.at[z], y_rs.at[z], y_peer))
    for j in (1, 3, 2):
        sent.append(
            send(mine_k, mine_k, h_ss.at[j], h_rs.at[j], (row_of(at_y(j), x), c))
        )
    x_sends(yh, mine_k)
    for delta in (1, -1, 2, -2, 3, -3, 4):
        zz = at_z(delta)
        sent.append(
            send(mine, mine, z_ss.at[zz], z_rs.at[z], (r, col_of(yl, zz, co)))
        )
    core_send(yl, z)
    place_queries(units, r, pos_s)
    result[...] = jnp.zeros_like(result)
    stat[...] = jnp.zeros_like(stat)
    dq_acc[...] = jnp.zeros_like(dq_acc)
    dkv_acc[...] = jnp.zeros_like(dkv_acc)
    y_arrive(0)
    z_arrive(1, -1)
    x_arrive(0)
    query_ready(z)
    scores_of(1, lambda i: (i, 0))
    z_arrive(2, -2)
    h_arrive(1)
    h_arrive(3)
    near_arrive()
    query_ready(at_z(1))
    query_ready(at_z(-1))
    scores_of(2, lambda i: (2 * i - 1, 0))
    h_arrive(2)
    z_arrive(3, -3)
    y_arrive(2, -2)
    query_ready(at_z(2))
    query_ready(at_z(-2))
    scores_of(2, lambda i: (4 * i - 2, 0))
    z_arrive(4)
    x_arrive(-1)
    scores_of(5, lambda i: (i - 2, -1))
    y_arrive(3, -3)
    x_arrive(1)
    scores_of(5, lambda i: (i - 2, 1))
    query_ready(at_z(3))
    query_ready(at_z(-3))
    scores_of(6, lambda i: (6 * (i // 3) - 3, i % 3 - 1))
    y_arrive(4)
    query_ready(at_z(4))
    scores_of(3, lambda i: (4, i - 1))
    x_arrive(2)
    scores_of(4, lambda i: ((2 * (i % 2) - 1) * ((i + 1) // 2), 2))
    stat_send(0, 1, -1, 2)
    scores_of(4, lambda i: ((2 * (i % 2) - 1) * ((i + 5) // 2), 2))
    stat_send(-2, 3, -3, 4)

    def stat_sent(o, _):
        @pl.when(owner_col(o) != c)
        def _():
            pltpu.make_async_remote_copy(
                src_ref=stat.at[o], dst_ref=inbox.at[c], send_sem=a_ss.at[o],
                recv_sem=a_rs.at[c], device_id=(r, owner_col(o)), device_id_type=MESH,
            ).wait_send()
        return 0

    owned = at_z(4)

    def give(partner):
        return pltpu.make_async_remote_copy(
            src_ref=result, dst_ref=done_stat.at[owned], send_sem=b_ss.at[partner[1]],
            recv_sem=b_rs.at[owned], device_id=partner, device_id_type=MESH,
        )

    @pl.when(owner_col(owned) == c)
    def _():
        for partner in reversed(partners):
            arrive(inbox.at[partner[1]], a_rs.at[partner[1]])
        lse = inbox[:, 0:LANE_ROWS, :]
        row_dot = inbox[:, LANE_ROWS:2 * LANE_ROWS, :]
        peak = jnp.max(lse, axis=0)
        part = jnp.exp2(lse - peak[None])
        total = jnp.sum(part, axis=0)
        result[0:LANE_ROWS, :] = peak + jnp.log2(total)
        result[LANE_ROWS:2 * LANE_ROWS, :] = jnp.sum(part * row_dot, axis=0) / total
        for partner in partners:
            give(partner).start()
        done_stat[owned] = result[...]

    def stat_take(zq):
        @pl.when(owner_col(zq) != c)
        def _():
            arrive(done_stat.at[zq], b_rs.at[zq])

    gather_sent = sent
    sent = []

    def grads_of(zqs, yks):
        pass_2_tile(
            [at_z(d) for d in zqs], [at_y(d) for d in yks],
            qd, kv, p_s, gw_s, peak_s, done_stat, dq_acc, dkv_acc,
        )

    def core_start(zz):
        sent.append(
            send(dq_acc.at[zz, :, 1 - co], sib_in.at[zz], rc_ss.at[zz], rc_rs.at[zz], sibling)
        )

    def core_end(zz):
        arrive(sib_in.at[zz], rc_rs.at[zz])
        return (dq_acc[zz, :, co] + sib_in[zz]) * SCALE

    def z_send(zz):
        zs[zz] = core_end(zz).astype(bf16)
        sent.append(
            send(zs.at[zz], zr.at[z], rz_ss.at[zz], rz_rs.at[z], (r, col_of(yl, zz, co)))
        )

    def z_end():
        total = core_end(z)
        for delta in (4, 3, -3, 2, -2, 1, -1):
            zz = at_z(delta)
            arrive(zr.at[zz], rz_rs.at[zz])
            total += zr[zz].astype(f32)
        q_sum[...] = total
        ys[...] = q_sum[1 - yl].astype(bf16)
        sent.append(send(ys, yr, ry_ss, ry_rs, y_peer))

    def y_end():
        arrive(yr, ry_rs)
        out[0] = (q_sum[yl] + yr[...].astype(f32)).astype(bf16)

    def scaled(a):
        return SCALE if a == 0 else 1.0

    def column_send(dy):
        for d in range(3):
            for a in range(2):
                term = dkv_acc[a, at_y(dy), at_x((1, -1, 2)[d])] * scaled(a)
                xs[dy % YH, d, a] = term.astype(bf16)
            sent.append(
                send(xs.at[dy % YH, d], xr.at[dy % YH, d], rx_ss.at[dy % YH, d],
                     rx_rs.at[dy % YH, d], x_next[d])
            )

    def column_end(dy):
        for d in range(3):
            arrive(xr.at[dy % YH, d], rx_rs.at[dy % YH, d])
        for a in range(2):
            total = dkv_acc[a, at_y(dy), x] * scaled(a)
            for d in range(3):
                total += xr[dy % YH, d, a].astype(f32)
            if dy == 0:
                kv_sum[a] = total
            else:
                hs[dy % YH, a] = total.astype(bf16)
        if dy != 0:
            j = dy % YH
            sent.append(
                send(hs.at[j], hr.at[j], rh_ss.at[j], rh_rs.at[j], (row_of(at_y(dy), x), c))
            )

    def high_end():
        for j in range(1, YH):
            arrive(hr.at[j], rh_rs.at[j])
        for a in range(2):
            total = kv_sum[a]
            for j in range(1, YH):
                total += hr[j, a].astype(f32)
            out[1 + a] = total.astype(bf16)

    for pair in ((4, 3), (-3, 2), (-2, 1), (-1, 0)):
        for delta in pair:
            stat_take(at_z(delta))
        grads_of(pair, [2])
    column_send(2)
    grads_of([4], [1, -1])
    grads_of([4], [0])
    core_start(at_z(4))
    grads_of([3, -3], [1, -1])
    z_send(at_z(4))
    grads_of([3, -3], [0])
    core_start(at_z(3))
    core_start(at_z(-3))

    for dy in (1, -1):
        grads_of([2, -2], [dy])
        if dy == 1:
            z_send(at_z(3))
            z_send(at_z(-3))
        grads_of([1, -1], [dy])
        grads_of([0], [dy])
        column_send(dy)
    column_end(2)
    grads_of([2, -2], [0])
    core_start(at_z(2))
    core_start(at_z(-2))
    grads_of([1, -1], [0])
    core_start(at_z(1))
    core_start(at_z(-1))
    z_send(at_z(2))
    z_send(at_z(-2))
    grads_of([0], [0])
    core_start(z)
    column_send(0)
    z_send(at_z(1))
    z_send(at_z(-1))
    column_end(1)
    column_end(-1)
    z_end()
    column_end(0)
    y_end()
    high_end()
    for copy in gather_sent + sent:
        copy.wait_send()
    lax.fori_loop(0, Z, stat_sent, 0)

    @pl.when(owner_col(owned) == c)
    def _():
        for partner in partners:
            give(partner).wait_send()


def parted(whole, *parts):
    for i, part in enumerate(parts):
        part[...] = whole[i]


def shards(queries, keys, values, out_grad, unit_order):
    vmem = pl.BlockSpec(memory_space=pltpu.VMEM)
    dma = pltpu.SemaphoreType.DMA
    shard = jax.ShapeDtypeStruct((SHARD, HD), bf16)
    tile = (SHARD, HD)
    groups = (Z, YH, X, 8, QT)
    whole = pl.pallas_call(
        kernel,
        out_shape=jax.ShapeDtypeStruct((3, SHARD, HD), bf16),
        in_specs=[pl.BlockSpec(memory_space=pl.ANY)] * 4 + [pl.BlockSpec(memory_space=pltpu.SMEM)],
        out_specs=vmem,
        scratch_shapes=[
            pltpu.VMEM((2, Z, YL, CORE) + tile, bf16),
            pltpu.VMEM((2, YH, X) + tile, bf16),
            pltpu.VMEM((Z, 8, QT), jnp.int32),
            pltpu.VMEM((Z, YH, KT, QT), f32),
            pltpu.VMEM((Z, YH, KT, QT), f32),
            pltpu.VMEM(groups, f32),
            pltpu.VMEM(groups, f32),
            pltpu.VMEM(groups, f32),
            pltpu.VMEM((Z, 8, UNIT), f32),
            pltpu.VMEM((COLS, 8, UNIT), f32),
            pltpu.VMEM((8, UNIT), f32),
            pltpu.VMEM((Z, 8, UNIT), f32),
            pltpu.VMEM((Z, YL, CORE) + tile, f32),
            pltpu.VMEM((2, YH, X) + tile, f32),
            pltpu.VMEM((Z, YL) + tile, f32),
            pltpu.VMEM((YL,) + tile, f32),
            pltpu.VMEM((Z, YL) + tile, bf16),
            pltpu.VMEM((Z, YL) + tile, bf16),
            pltpu.VMEM(tile, bf16),
            pltpu.VMEM(tile, bf16),
            pltpu.VMEM((YH, 3, 2) + tile, bf16),
            pltpu.VMEM((YH, 3, 2) + tile, bf16),
            pltpu.VMEM((2,) + tile, f32),
            pltpu.VMEM((YH, 2) + tile, bf16),
            pltpu.VMEM((YH, 2) + tile, bf16),
            dma((Z,)), dma((Z,)),
            dma((Z,)), dma((Z,)),
            dma((2,)), dma((2,)),
            dma((YL, Z)), dma((YL, Z)),
            dma((YH,)), dma((YH,)),
            dma((3, YH)), dma((3, YH)),
            dma((Z,)), dma((COLS,)),
            dma((COLS,)), dma((Z,)),
            dma((4,)),
            dma((Z,)), dma((Z,)),
            dma((Z,)), dma((Z,)),
            dma, dma,
            dma((YH, 3)), dma((YH, 3)),
            dma((YH,)), dma((YH,)),
        ],
        compiler_params=pltpu.CompilerParams(
            collective_id=0, has_side_effects=True, vmem_limit_bytes=60 * 2**20
        ),
    )(queries, keys, values, out_grad, unit_order)
    return pl.pallas_call(
        parted,
        out_shape=(shard, shard, shard),
        in_specs=[vmem],
        out_specs=(vmem, vmem, vmem),
    )(whole)


def solution(mesh):
    placed = (
        P(("row", "col"), None),
        P(("col", "row"), None),
        P(("col", "row"), None),
        P(("row", "col"), None),
        P(),
    )
    return jax.shard_map(
        shards,
        mesh=mesh,
        in_specs=placed,
        out_specs=(P(("row", "col"), None), P(("col", "row"), None), P(("col", "row"), None)),
        check_vma=False,
    )
```

```python
import functools
import math

import jax
import jax.numpy as jnp
from jax import lax
from jax.experimental import pallas as pl
from jax.experimental.pallas import tpu as pltpu
from jax.sharding import PartitionSpec as P

UNIT = 128
HD = 128
SHARD = 96
YH, X, YL, Z, CORE = 4, 4, 2, 8, 2
ROWS, COLS = YH * X, YL * Z * CORE
QN, KN = COLS * SHARD, ROWS * SHARD
QUNITS, KUNITS = QN // UNIT, KN // UNIT
QT = YL * CORE * SHARD
KT = X * SHARD
LANE_ROWS = QT // UNIT
MASK_ROWS = 32
SCALE = 1.0 / math.sqrt(HD)
LOG2_SCALE = math.log2(math.e) * SCALE
masked_score = -1e30
lowest_peak = -1e29
least_total = 1e-30

f32 = jnp.float32
bf16 = jnp.bfloat16
MESH = pl.DeviceIdType.MESH
contract_last = (((1,), (1,)), ((), ()))
contract_first = (((0,), (0,)), ((), ()))


def wrap(value, size):
    return lax.rem(value + size, size)


def owner_col(o):
    far = (o + Z // 2) % Z
    return (o % 2) * (Z * CORE) + far * CORE + (o // 2) % 2


def place_queries(units, r, pos_s):
    lane = lax.broadcasted_iota(jnp.int32, (8, QT), 1)
    half = CORE * SHARD
    side = lane // half
    for zz in range(Z):
        token = side * (Z * half) + zz * half + (lane - side * half)
        unit, inside = token // UNIT, token % UNIT
        base = jnp.zeros((8, QT), jnp.int32)
        for a in range(YL):
            first = (a * Z + zz) * half // UNIT
            for u in (first, first + 1):
                base = jnp.where(unit == u, units[r * QUNITS + u], base)
        pos_s[zz] = base * UNIT + inside


def pass_1_tile(units, c, zq, yk, qd, kv, pos_s, p_s, gw_s, peak_s, total_s, dot_s):
    query, grad = qd[0, zq].reshape(QT, HD), qd[1, zq].reshape(QT, HD)
    sub = lax.broadcasted_iota(jnp.int32, (MASK_ROWS // 8, 8, QT), 0) * 8 + lax.broadcasted_iota(
        jnp.int32, (MASK_ROWS // 8, 8, QT), 1
    )
    query_pos = pos_s[zq]
    keys, values = kv[0, yk].reshape(KT, HD), kv[1, yk].reshape(KT, HD)
    all_scores = lax.dot_general(keys, query, contract_last, preferred_element_type=f32)
    all_grads = lax.dot_general(values, grad, contract_last, preferred_element_type=f32)
    for place in range(X):
        rows = slice(place * SHARD, (place + 1) * SHARD)
        scores = all_scores[rows].reshape(SHARD // 8, 8, QT)
        grad_weights = all_grads[rows]
        parts = []
        for b in range(SHARD // MASK_ROWS):
            token = (yk * X + place) * SHARD + b * MASK_ROWS
            key_pos = units[c * KUNITS + token // UNIT] * UNIT + token % UNIT
            part = scores[b * MASK_ROWS // 8:(b + 1) * MASK_ROWS // 8]
            parts.append(
                jnp.where(sub <= (query_pos - key_pos)[None], part * LOG2_SCALE, masked_score)
            )
        scores = jnp.concatenate(parts, axis=0)
        peak = jnp.maximum(jnp.max(scores, axis=0), lowest_peak)
        expos = jnp.exp2(scores - peak[None])
        peak_s[zq, yk, place] = peak
        total_s[zq, yk, place] = jnp.sum(expos, axis=0)
        dot_s[zq, yk, place] = jnp.sum(expos * grad_weights.reshape(SHARD // 8, 8, QT), axis=0)
        p_s[zq, yk, rows, :] = expos.reshape(SHARD, QT)
        gw_s[zq, yk, rows, :] = grad_weights


def row_statistics(zq, peak_s, total_s, dot_s, stat):
    peaks = peak_s[zq].reshape(X * YH, 8, QT)
    peak = jnp.max(jnp.max(peaks, axis=0), axis=0, keepdims=True)
    factors = jnp.exp2(peaks - peak[None])
    total = jnp.sum(total_s[zq].reshape(X * YH, 8, QT) * factors, axis=0)
    dot = jnp.sum(dot_s[zq].reshape(X * YH, 8, QT) * factors, axis=0)
    total = jnp.maximum(jnp.sum(total, axis=0, keepdims=True), least_total)
    dot = jnp.sum(dot, axis=0, keepdims=True)
    lse = peak + jnp.log2(total)
    row_dot = dot / total
    for i in range(LANE_ROWS):
        lanes = slice(i * UNIT, (i + 1) * UNIT)
        stat[zq, i:i + 1, :] = lse[:, lanes]
        stat[zq, LANE_ROWS + i:LANE_ROWS + i + 1, :] = row_dot[:, lanes]


def pass_2_tile(zqs, yks, qd, kv, p_s, gw_s, peak_s, done_stat, dq_acc, dkv_acc, fresh=False):
    weights, grad_scores = [[] for _ in yks], [[] for _ in yks]
    for zq in zqs:
        lse = jnp.concatenate([done_stat[zq, i:i + 1, :] for i in range(LANE_ROWS)], axis=1)
        row_dot = jnp.concatenate(
            [done_stat[zq, LANE_ROWS + i:LANE_ROWS + i + 1, :] for i in range(LANE_ROWS)], axis=1
        )
        for j, yk in enumerate(yks):
            w_parts, g_parts = [], []
            for place in range(X):
                rows = slice(place * SHARD, (place + 1) * SHARD)
                factor = jnp.exp2(peak_s[zq, yk, place] - lse)
                w = p_s[zq, yk, rows, :].reshape(SHARD // 8, 8, QT) * factor[None]
                g = w * (gw_s[zq, yk, rows, :].reshape(SHARD // 8, 8, QT) - row_dot[None])
                w_parts.append(w.reshape(SHARD, QT).astype(bf16))
                g_parts.append(g.reshape(SHARD, QT).astype(bf16))
            weights[j].append(jnp.concatenate(w_parts, axis=0))
            grad_scores[j].append(jnp.concatenate(g_parts, axis=0))
    weights = [jnp.concatenate(row, axis=1) for row in weights]
    grad_scores = [jnp.concatenate(row, axis=1) for row in grad_scores]
    query = jnp.concatenate([qd[0, zq].reshape(QT, HD) for zq in zqs], axis=0)
    grad = jnp.concatenate([qd[1, zq].reshape(QT, HD) for zq in zqs], axis=0)
    for j, yk in enumerate(yks):
        value_part = jnp.dot(weights[j], grad, preferred_element_type=f32)
        key_part = jnp.dot(grad_scores[j], query, preferred_element_type=f32)
        dkv_acc[1, yk] += value_part.reshape(X, SHARD, HD)
        dkv_acc[0, yk] += key_part.reshape(X, SHARD, HD)
    query_part = lax.dot_general(
        jnp.concatenate(grad_scores, axis=0),
        jnp.concatenate([kv[0, yk].reshape(KT, HD) for yk in yks], axis=0),
        contract_first, preferred_element_type=f32,
    )
    for i, zq in enumerate(zqs):
        dq_acc[zq] += query_part[i * QT:(i + 1) * QT].reshape(YL, CORE, SHARD, HD)


def kernel(
    q_ref, k_ref, v_ref, g_ref, units,
    out,
    qd, kv, pos_s, p_s, gw_s, peak_s, total_s, dot_s, stat, inbox, result, done_stat,
    dq_acc, dkv_acc, sib_in, q_sum, zs, zr, ys, yr, xs, xr, kv_sum, hs, hr,
    y_ss, y_rs, z_ss, z_rs, n_ss, n_rs, c_ss, c_rs, h_ss, h_rs, x_ss, x_rs,
    a_ss, a_rs, b_ss, b_rs,
    own_s, rc_ss, rc_rs, rz_ss, rz_rs, ry_ss, ry_rs, rx_ss, rx_rs, rh_ss, rh_rs,
):
    r = lax.axis_index("row")
    c = lax.axis_index("col")
    yh, x = r // X, r % X
    yl, z, co = c // (Z * CORE), (c // CORE) % Z, c % CORE

    def col_of(a, b, d):
        return a * (Z * CORE) + b * CORE + d

    def row_of(a, b):
        return a * X + b

    def at_z(delta):
        return wrap(z + delta, Z)

    def at_x(delta):
        return wrap(x + delta, X)

    def at_y(delta):
        return wrap(yh + delta, YH)

    sibling = (r, col_of(yl, z, 1 - co))
    y_peer = (r, col_of(1 - yl, z, co))
    z_next = [(r, col_of(yl, at_z(1), co)), (r, col_of(yl, at_z(-1), co))]
    x_next = [(row_of(yh, at_x(1)), c), (row_of(yh, at_x(-1)), c), (row_of(yh, at_x(2)), c)]
    way = (1, -1)

    def send(src, dst, send_sem, recv_sem, device):
        copy = pltpu.make_async_remote_copy(
            src_ref=src, dst_ref=dst, send_sem=send_sem, recv_sem=recv_sem,
            device_id=device, device_id_type=MESH,
        )
        copy.start()
        return copy

    def arrive(dst, recv_sem):
        pltpu.make_async_remote_copy(
            src_ref=dst, dst_ref=dst, send_sem=recv_sem, recv_sem=recv_sem,
            device_id=sibling, device_id_type=MESH,
        ).wait_recv()

    barrier = pltpu.get_barrier_semaphore()

    partners = [
        (r, col_of(wrap(yl + a, YL), at_z(delta), wrap(co + b, CORE)))
        for delta in (4, 3, -3, 2, -2, 1, -1, 0) for a in (1, 0) for b in (1, 0)
        if (delta, a, b) != (0, 0, 0)
    ]
    for device in partners:
        pl.semaphore_signal(barrier, inc=1, device_id=device, device_id_type=MESH)
    for device in x_next:
        pl.semaphore_signal(barrier, inc=1, device_id=device, device_id_type=MESH)
    for j in range(1, YH):
        pl.semaphore_signal(
            barrier, inc=1, device_id=(row_of(at_y(j), x), c), device_id_type=MESH
        )

    own = [
        pltpu.make_async_copy(src, dst, own_s.at[i])
        for i, (src, dst) in enumerate((
            (q_ref, qd.at[0, z, yl, co]), (g_ref, qd.at[1, z, yl, co]),
            (k_ref, kv.at[0, yh, x]), (v_ref, kv.at[1, yh, x]),
        ))
    ]
    for copy in own:
        copy.start()

    def q_slot(a, b, d):
        return qd.at[:, b, a, d]

    def k_slot(high, xx):
        return kv.at[:, high, xx]

    for copy in own:
        copy.wait()
    pl.semaphore_wait(barrier, COLS - 1 + 3 + YH - 1)

    sent = []

    def core_send(side, zz):
        slot = q_slot(side, zz, co)
        sent.append(send(slot, slot, c_ss.at[side, zz], c_rs.at[side, zz], sibling))

    def x_sends(high, slot):
        for d in range(3):
            sent.append(send(slot, slot, x_ss.at[d, high], x_rs.at[d, high], x_next[d]))

    def z_arrive(*deltas):
        for delta in deltas:
            zz = at_z(delta)
            slot = q_slot(yl, zz, co)
            arrive(slot, z_rs.at[zz])
            if abs(delta) > 1:
                sent.append(send(slot, slot, y_ss.at[zz], y_rs.at[zz], y_peer))
            core_send(yl, zz)

    def y_arrive(*deltas):
        for delta in deltas:
            zz = at_z(delta)
            slot = q_slot(1 - yl, zz, co)
            arrive(slot, y_rs.at[zz])
            if delta == 0:
                for d in range(2):
                    sent.append(send(slot, slot, n_ss.at[d], n_rs.at[d], z_next[d]))
            core_send(1 - yl, zz)

    def near_arrive():
        for d in range(2):
            zz = at_z(-way[d])
            arrive(q_slot(1 - yl, zz, co), n_rs.at[d])
            core_send(1 - yl, zz)

    def h_arrive(j):
        high = at_y(-j)
        slot = k_slot(high, x)
        arrive(slot, h_rs.at[j])
        x_sends(high, slot)

    def x_arrive(delta):
        high = at_y(delta)
        for d in range(3):
            arrive(k_slot(high, at_x((-1, 1, 2)[d])), x_rs.at[d, high])

    def query_ready(zz):
        for side in range(2):
            arrive(q_slot(side, zz, 1 - co), c_rs.at[side, zz])

    def scores_of(count, where):
        def one(i, _):
            dz, dy = where(i)
            pass_1_tile(
                units, c, at_z(dz), at_y(dy), qd, kv, pos_s, p_s, gw_s, peak_s, total_s, dot_s
            )
            return 0

        lax.fori_loop(0, count, one, 0, unroll=count)

    def stat_send(*deltas):
        for delta in deltas:
            row_statistics(at_z(delta), peak_s, total_s, dot_s, stat)
        for delta in deltas:
            zq = at_z(delta)
            target = owner_col(zq)

            @pl.when(target != c)
            def _():
                send(stat.at[zq], inbox.at[c], a_ss.at[zq], a_rs.at[c], (r, target))

            @pl.when(target == c)
            def _():
                inbox[c] = stat[zq]

    mine = q_slot(yl, z, co)
    mine_k = k_slot(yh, x)
    sent.append(send(mine, mine, y_ss.at[z], y_rs.at[z], y_peer))
    for j in (1, 3, 2):
        sent.append(
            send(mine_k, mine_k, h_ss.at[j], h_rs.at[j], (row_of(at_y(j), x), c))
        )
    x_sends(yh, mine_k)
    for delta in (1, -1, 2, -2, 3, -3, 4):
        zz = at_z(delta)
        sent.append(
            send(mine, mine, z_ss.at[zz], z_rs.at[z], (r, col_of(yl, zz, co)))
        )
    core_send(yl, z)
    place_queries(units, r, pos_s)
    result[...] = jnp.zeros_like(result)
    stat[...] = jnp.zeros_like(stat)
    dq_acc[...] = jnp.zeros_like(dq_acc)
    dkv_acc[...] = jnp.zeros_like(dkv_acc)
    y_arrive(0)
    z_arrive(1, -1)
    x_arrive(0)
    query_ready(z)
    scores_of(1, lambda i: (i, 0))
    z_arrive(2, -2)
    h_arrive(1)
    h_arrive(3)
    near_arrive()
    query_ready(at_z(1))
    query_ready(at_z(-1))
    scores_of(2, lambda i: (2 * i - 1, 0))
    h_arrive(2)
    z_arrive(3, -3)
    y_arrive(2, -2)
    query_ready(at_z(2))
    query_ready(at_z(-2))
    scores_of(2, lambda i: (4 * i - 2, 0))
    z_arrive(4)
    x_arrive(-1)
    scores_of(5, lambda i: (i - 2, -1))
    y_arrive(3, -3)
    x_arrive(1)
    scores_of(5, lambda i: (i - 2, 1))
    query_ready(at_z(3))
    query_ready(at_z(-3))
    scores_of(6, lambda i: (6 * (i // 3) - 3, i % 3 - 1))
    y_arrive(4)
    query_ready(at_z(4))
    scores_of(3, lambda i: (4, i - 1))
    x_arrive(2)
    scores_of(4, lambda i: ((2 * (i % 2) - 1) * ((i + 1) // 2), 2))
    stat_send(0, 1, -1, 2)
    scores_of(4, lambda i: ((2 * (i % 2) - 1) * ((i + 5) // 2), 2))
    stat_send(-2, 3, -3, 4)

    def stat_sent(o, _):
        @pl.when(owner_col(o) != c)
        def _():
            pltpu.make_async_remote_copy(
                src_ref=stat.at[o], dst_ref=inbox.at[c], send_sem=a_ss.at[o],
                recv_sem=a_rs.at[c], device_id=(r, owner_col(o)), device_id_type=MESH,
            ).wait_send()
        return 0

    owned = at_z(4)

    def give(partner):
        return pltpu.make_async_remote_copy(
            src_ref=result, dst_ref=done_stat.at[owned], send_sem=b_ss.at[partner[1]],
            recv_sem=b_rs.at[owned], device_id=partner, device_id_type=MESH,
        )

    @pl.when(owner_col(owned) == c)
    def _():
        for partner in reversed(partners):
            arrive(inbox.at[partner[1]], a_rs.at[partner[1]])
        lse = inbox[:, 0:LANE_ROWS, :]
        row_dot = inbox[:, LANE_ROWS:2 * LANE_ROWS, :]
        peak = jnp.max(lse, axis=0)
        part = jnp.exp2(lse - peak[None])
        total = jnp.sum(part, axis=0)
        result[0:LANE_ROWS, :] = peak + jnp.log2(total)
        result[LANE_ROWS:2 * LANE_ROWS, :] = jnp.sum(part * row_dot, axis=0) / total
        for partner in partners:
            give(partner).start()
        done_stat[owned] = result[...]

    def stat_take(zq):
        @pl.when(owner_col(zq) != c)
        def _():
            arrive(done_stat.at[zq], b_rs.at[zq])

    gather_sent = sent
    sent = []

    def grads_of(zqs, yks):
        pass_2_tile(
            [at_z(d) for d in zqs], [at_y(d) for d in yks],
            qd, kv, p_s, gw_s, peak_s, done_stat, dq_acc, dkv_acc,
        )

    def core_start(zz):
        sent.append(
            send(dq_acc.at[zz, :, 1 - co], sib_in.at[zz], rc_ss.at[zz], rc_rs.at[zz], sibling)
        )

    def core_end(zz):
        arrive(sib_in.at[zz], rc_rs.at[zz])
        return (dq_acc[zz, :, co] + sib_in[zz]) * SCALE

    def z_send(zz):
        zs[zz] = core_end(zz).astype(bf16)
        sent.append(
            send(zs.at[zz], zr.at[z], rz_ss.at[zz], rz_rs.at[z], (r, col_of(yl, zz, co)))
        )

    def z_end():
        total = core_end(z)
        for delta in (4, 3, -3, 2, -2, 1, -1):
            zz = at_z(delta)
            arrive(zr.at[zz], rz_rs.at[zz])
            total += zr[zz].astype(f32)
        q_sum[...] = total
        ys[...] = q_sum[1 - yl].astype(bf16)
        sent.append(send(ys, yr, ry_ss, ry_rs, y_peer))

    def y_end():
        arrive(yr, ry_rs)
        out[0] = (q_sum[yl] + yr[...].astype(f32)).astype(bf16)

    def scaled(a):
        return SCALE if a == 0 else 1.0

    def column_send(dy):
        for d in range(3):
            for a in range(2):
                term = dkv_acc[a, at_y(dy), at_x((1, -1, 2)[d])] * scaled(a)
                xs[dy % YH, d, a] = term.astype(bf16)
            sent.append(
                send(xs.at[dy % YH, d], xr.at[dy % YH, d], rx_ss.at[dy % YH, d],
                     rx_rs.at[dy % YH, d], x_next[d])
            )

    def column_end(dy):
        for d in range(3):
            arrive(xr.at[dy % YH, d], rx_rs.at[dy % YH, d])
        for a in range(2):
            total = dkv_acc[a, at_y(dy), x] * scaled(a)
            for d in range(3):
                total += xr[dy % YH, d, a].astype(f32)
            if dy == 0:
                kv_sum[a] = total
            else:
                hs[dy % YH, a] = total.astype(bf16)
        if dy != 0:
            j = dy % YH
            sent.append(
                send(hs.at[j], hr.at[j], rh_ss.at[j], rh_rs.at[j], (row_of(at_y(dy), x), c))
            )

    def high_end():
        for j in range(1, YH):
            arrive(hr.at[j], rh_rs.at[j])
        for a in range(2):
            total = kv_sum[a]
            for j in range(1, YH):
                total += hr[j, a].astype(f32)
            out[1 + a] = total.astype(bf16)

    for pair in ((4, 3), (-3, 2), (-2, 1), (-1, 0)):
        for delta in pair:
            stat_take(at_z(delta))
        grads_of(pair, [2])
    column_send(2)
    grads_of([4], [1, -1])
    grads_of([4], [0])
    core_start(at_z(4))
    grads_of([3, -3], [1, -1])
    z_send(at_z(4))
    grads_of([3, -3], [0])
    core_start(at_z(3))
    core_start(at_z(-3))

    for dy in (1, -1):
        grads_of([2, -2, 1, -1, 0], [dy])
        column_send(dy)
        if dy == 1:
            z_send(at_z(3))
            z_send(at_z(-3))
    column_end(2)
    grads_of([2, -2], [0])
    core_start(at_z(2))
    core_start(at_z(-2))
    grads_of([1, -1], [0])
    core_start(at_z(1))
    core_start(at_z(-1))
    z_send(at_z(2))
    z_send(at_z(-2))
    grads_of([0], [0])
    core_start(z)
    column_send(0)
    z_send(at_z(1))
    z_send(at_z(-1))
    column_end(1)
    column_end(-1)
    z_end()
    column_end(0)
    y_end()
    high_end()
    for copy in gather_sent + sent:
        copy.wait_send()
    lax.fori_loop(0, Z, stat_sent, 0)

    @pl.when(owner_col(owned) == c)
    def _():
        for partner in partners:
            give(partner).wait_send()


def parted(whole, *parts):
    for i, part in enumerate(parts):
        part[...] = whole[i]


def shards(queries, keys, values, out_grad, unit_order):
    vmem = pl.BlockSpec(memory_space=pltpu.VMEM)
    dma = pltpu.SemaphoreType.DMA
    shard = jax.ShapeDtypeStruct((SHARD, HD), bf16)
    tile = (SHARD, HD)
    groups = (Z, YH, X, 8, QT)
    whole = pl.pallas_call(
        kernel,
        out_shape=jax.ShapeDtypeStruct((3, SHARD, HD), bf16),
        in_specs=[pl.BlockSpec(memory_space=pl.ANY)] * 4 + [pl.BlockSpec(memory_space=pltpu.SMEM)],
        out_specs=vmem,
        scratch_shapes=[
            pltpu.VMEM((2, Z, YL, CORE) + tile, bf16),
            pltpu.VMEM((2, YH, X) + tile, bf16),
            pltpu.VMEM((Z, 8, QT), jnp.int32),
            pltpu.VMEM((Z, YH, KT, QT), f32),
            pltpu.VMEM((Z, YH, KT, QT), f32),
            pltpu.VMEM(groups, f32),
            pltpu.VMEM(groups, f32),
            pltpu.VMEM(groups, f32),
            pltpu.VMEM((Z, 8, UNIT), f32),
            pltpu.VMEM((COLS, 8, UNIT), f32),
            pltpu.VMEM((8, UNIT), f32),
            pltpu.VMEM((Z, 8, UNIT), f32),
            pltpu.VMEM((Z, YL, CORE) + tile, f32),
            pltpu.VMEM((2, YH, X) + tile, f32),
            pltpu.VMEM((Z, YL) + tile, f32),
            pltpu.VMEM((YL,) + tile, f32),
            pltpu.VMEM((Z, YL) + tile, bf16),
            pltpu.VMEM((Z, YL) + tile, bf16),
            pltpu.VMEM(tile, bf16),
            pltpu.VMEM(tile, bf16),
            pltpu.VMEM((YH, 3, 2) + tile, bf16),
            pltpu.VMEM((YH, 3, 2) + tile, bf16),
            pltpu.VMEM((2,) + tile, f32),
            pltpu.VMEM((YH, 2) + tile, bf16),
            pltpu.VMEM((YH, 2) + tile, bf16),
            dma((Z,)), dma((Z,)),
            dma((Z,)), dma((Z,)),
            dma((2,)), dma((2,)),
            dma((YL, Z)), dma((YL, Z)),
            dma((YH,)), dma((YH,)),
            dma((3, YH)), dma((3, YH)),
            dma((Z,)), dma((COLS,)),
            dma((COLS,)), dma((Z,)),
            dma((4,)),
            dma((Z,)), dma((Z,)),
            dma((Z,)), dma((Z,)),
            dma, dma,
            dma((YH, 3)), dma((YH, 3)),
            dma((YH,)), dma((YH,)),
        ],
        compiler_params=pltpu.CompilerParams(
            collective_id=0, has_side_effects=True, vmem_limit_bytes=60 * 2**20
        ),
    )(queries, keys, values, out_grad, unit_order)
    return pl.pallas_call(
        parted,
        out_shape=(shard, shard, shard),
        in_specs=[vmem],
        out_specs=(vmem, vmem, vmem),
    )(whole)


def solution(mesh):
    placed = (
        P(("row", "col"), None),
        P(("col", "row"), None),
        P(("col", "row"), None),
        P(("row", "col"), None),
        P(),
    )
    return jax.shard_map(
        shards,
        mesh=mesh,
        in_specs=placed,
        out_specs=(P(("row", "col"), None), P(("col", "row"), None), P(("col", "row"), None)),
        check_vma=False,
    )
```
